512 devices in a mesh: occ: 16 (over y_lo, x, core), vir: 32 (over z, y_hi).
Axes of the slice: x: 4, y: 4 (y_hi: 2, y_lo: 2; y = y_hi * 2 + y_lo), z: 16, core: 2. Of those that a mesh axis runs over, the one named last changes fastest.
Arguments:
- amps: bfloat16 [16384, 3072], P('occ', 'vir'), may hold values from -6 to 6
- ints: bfloat16 [3072, 16384], P(None, 'vir'), may hold values from -0.109375 to 0.109375
- amp_mask: int32 [512, 6], P('occ'), may hold values 0 or 1
- keep_mask: int32 [512, 32], P('occ', 'vir'), may hold values 0 or 1
- owners: int32 [512, 1], P('occ'), may hold values from 0 to 15; in each aligned block of 32 rows (0 to 31, 32 to 63, ...) at most 4 rows name the same one
- occ_energy: bfloat16 [16384], P('occ'), may hold values from -2 to -0.5
- vir_energy: float32 [16384], P('vir'), may hold values from 0.5 to 3
- mix: bfloat16 [16, 32, 32], P('occ'), may hold values from -4 to 4
Outputs:
- owned: bfloat16 [1024, 32, 16384], P('occ', None, 'vir')
The draws below stay inside these ranges and needn't reach their ends.
Inputs may be any that keep to these rules, and one draw needn't show every extreme that they name: `owners`: in the row tiles of one index of occ no owner appears more than 4 times; in every draw some owner appears exactly 4 times in some device's tiles.
All inputs are finite; a program needn't handle non-finite values. No bound on the sum of `amp_mask` or of `keep_mask` on one device may be relied on, other than what follows from the above.
Results may differ from the reference program's by a relative error of at most 0.0049.
Values may be sent and summed in bfloat16 or wider, within the bound.
No kernel may reach another device: no remote copies, remote signals or barrier semaphores. Data moves between devices by JAX's collectives and lax.ppermute only.
A program may use at most 64 MiB of HBM per device.

```python
import math
import jax
import jax.numpy as jnp
import numpy as np

TILE = 512
KT = 6
RT = 32
TILES_DEV = 32
COL_DEV = 512
K = 3072
ROW_TILES = 512
ROWS = 16384
COLS = 16384
OWNERS = 16
CAP = 4
SLOTS = 1024
N_VIR = 32


def draw_mix(key, part):
    noise = jax.random.normal(key, (OWNERS, RT, RT), jnp.float32)
    noise = jnp.clip(noise, -5.0, 5.0)
    return (jnp.eye(RT, dtype=jnp.float32)[None] + 0.6 * noise / math.sqrt(RT)).astype(jnp.bfloat16)


def set_ends(entries, own_key, least, largest):
    place = [jax.random.randint(jax.random.fold_in(own_key, axis), (), 0, length) for axis, length in enumerate(entries.shape)]
    widest = entries.shape.index(max(entries.shape))
    next_to = place[:widest] + [(place[widest] + 1) % entries.shape[widest]] + place[widest + 1:]
    return entries.at[tuple(place)].set(least).at[tuple(next_to)].set(largest)


def steps_of(rng, extent, pieces, least, top_value):
    def one(dim, blocks):
        draws = jax.random.uniform(jax.random.fold_in(jax.random.fold_in(rng, 6), dim), (blocks,), jnp.float32, least / len(pieces), top_value / len(pieces))
        return jnp.repeat(jnp.exp(draws), extent[dim] // blocks).reshape((-1,) + (1,) * (len(extent) - dim - 1))

    factor_of = one(*pieces[0])
    for cut in pieces[1:]:
        factor_of = factor_of * one(*cut)
    return factor_of


def routed_block(rng, own, number, rows, number_of, top, limit, slope):
    order = jax.random.permutation(rng, number_of)
    heavy_load, common = portions_of(number_of, rows * top, limit, slope, True), portions_of(number_of, rows * top, limit, slope, False)
    places = jnp.arange(number_of)

    def named(sizes, turn):
        used = int((sizes > 0).sum())
        fixed = max(1, used // 4)
        moved = fixed + (places - fixed + turn * (used - fixed)) % max(1, number_of - fixed)
        return jnp.zeros((number_of,), jnp.int32).at[order[jnp.where(places < fixed, places, moved)]].set(jnp.asarray(sizes, jnp.int32))

    sizes = jnp.where(number % 4 == 0, named(heavy_load, number // 4), named(common, number - number // 4 - 1))
    mixed = jax.random.permutation(jax.random.fold_in(own, 3), number_of)
    giver, receiver = mixed[0:number_of // 2 * 2:2], mixed[1:number_of // 2 * 2:2]
    margin = jnp.minimum(sizes[giver] - 1, limit - sizes[receiver]) // 2
    margin = jnp.where((giver == order[0]) | (receiver == order[0]) | (sizes[receiver] == 0), 0, jnp.maximum(margin, 0))
    moved = jax.random.randint(jax.random.fold_in(own, 4), (number_of // 2,), 0, 1 << 20) % (margin + 1)
    sizes = sizes.at[giver].add(-moved).at[receiver].add(moved)
    members = jnp.searchsorted(jnp.cumsum(sizes), jnp.arange(rows * top), side="right").astype(jnp.int32)
    table = members.reshape(top, rows).T
    table = table[jax.random.permutation(jax.random.fold_in(own, 1), rows)]
    turn = jax.random.randint(jax.random.fold_in(own, 2), (rows, 1), 0, top)
    return jnp.take_along_axis(table, (jnp.arange(top)[None, :] + turn) % top, axis=1)


def portions_of(amount, total, bound, slope, full):
    loads = [(1 << 20) // math.isqrt(grade ** slope) + 1 for grade in range(1, amount + 1)]
    largest = bound if full else min(bound, max(-(-total // amount), total * loads[0] // sum(loads)))
    least = 1 if total - largest >= amount - 1 else 0
    holding, rest = [largest] + [least] * (amount - 1), total - largest - least * (amount - 1)
    while rest > 0:
        movable = [i for i in range(1, amount) if holding[i] < largest] or [i for i in range(1, amount) if holding[i] < bound]
        whole, left = sum([loads[i] for i in movable]), rest
        for i in movable:
            extra = min(bound - holding[i], max(1, left * loads[i] // whole), rest)
            holding[i] = holding[i] + extra
            rest = rest - extra
    return np.array(holding)


def centred(own_key, extent, deviation, limit, shards=(), held_as=jnp.bfloat16):
    values = deviation * jax.random.normal(own_key, extent, jnp.float32)
    if shards:
        values = values * steps_of(own_key, extent, shards, -0.22, 0.18)
    return jnp.clip(values, -limit, limit).astype(held_as)


def setup_inputs(seed: int = 0) -> dict:
    keys = jax.random.split(jax.random.key(seed), 9)
    amps = centred(keys[0], (ROWS, K), 1.0, 6.0, ((0, 16), (1, 32)))
    ints = centred(keys[1], (K, COLS), K ** -0.5, 0.109375, ((1, 32),))
    amp_mask = set_ends((jax.random.randint(keys[2], (ROW_TILES, KT), 0, 3) < 2).astype(jnp.int32), jax.random.fold_in(keys[2], 1), 0, 1)
    keep_mask = set_ends((jax.random.randint(keys[3], (ROW_TILES, N_VIR), 0, 4) < 3).astype(jnp.int32), jax.random.fold_in(keys[3], 1), 0, 1)
    owners_keys = jax.random.split(jax.random.fold_in(keys[4], 1), ROW_TILES // TILES_DEV)
    owners_turns = jax.random.permutation(jax.random.fold_in(keys[4], 3), ROW_TILES // TILES_DEV)
    owners = jax.vmap(lambda own, number: routed_block(jax.random.fold_in(keys[4], 2), own, number, TILES_DEV, OWNERS, 1, CAP, 2))(owners_keys, owners_turns).reshape((ROW_TILES, 1))
    occ_energy = jnp.clip(-2.0 + 1.5 * jax.random.uniform(keys[5], (ROWS,), jnp.float32) ** steps_of(keys[5], (ROWS,), ((0, 16),), -0.2, 0.2), -2.0, -0.5).astype(jnp.bfloat16)
    vir_energy = jnp.clip(0.5 + 2.5 * jax.random.uniform(keys[6], (COLS,), jnp.float32) ** steps_of(keys[6], (COLS,), ((0, 32),), -0.2, 0.2), 0.5, 3.0)
    mix = draw_mix(jax.random.fold_in(keys[8], 71), 0)
    return {"amps": amps, "ints": ints, "amp_mask": amp_mask, "keep_mask": keep_mask, "owners": owners, "occ_energy": occ_energy, "vir_energy": vir_energy, "mix": mix}


def reference(amps, ints, amp_mask, keep_mask, owners, occ_energy, vir_energy, mix):
    k_tile = jnp.arange(K) // TILE
    amp_cols = amp_mask.astype(jnp.float32)[:, k_tile]
    amp_full = jnp.repeat(amp_cols, RT, axis=0)
    masked = (amps.astype(jnp.float32) * amp_full).astype(jnp.bfloat16)
    ladder = jnp.dot(masked, ints, preferred_element_type=jnp.float32).astype(jnp.bfloat16)
    keep_full = jnp.repeat(jnp.repeat(keep_mask.astype(jnp.float32), RT, axis=0), COL_DEV, axis=1)
    kept = (ladder.astype(jnp.float32) * keep_full).astype(jnp.bfloat16)
    tiles = kept.reshape(ROW_TILES, RT, COLS)
    destination = owners[:, 0]
    weights = mix[destination].astype(jnp.float32)
    mixed_rows = jnp.einsum("tij,tjc->tic", weights, tiles.astype(jnp.float32))
    denominator = vir_energy[None, None, :] - occ_energy.astype(jnp.float32).reshape(ROW_TILES, RT)[:, :, None]
    update = (mixed_rows / denominator).astype(jnp.bfloat16)
    grouped = destination.reshape(OWNERS, TILES_DEV)
    same_owner = grouped[:, :, None] == grouped[:, None, :]
    earlier = jnp.arange(TILES_DEV)[:, None] > jnp.arange(TILES_DEV)[None, :]
    position = jnp.sum((same_owner & earlier[None]).astype(jnp.int32), axis=2).reshape(-1)
    source = (jnp.arange(ROW_TILES) // TILES_DEV).astype(jnp.int32)
    slot_index = (destination * (OWNERS * CAP) + source * CAP + position).astype(jnp.int32)
    owned = jnp.zeros((SLOTS, RT, COLS), jnp.bfloat16).at[slot_index].set(update)
    return owned
```

```python
import jax
import jax.numpy as jnp
from jax import lax
from jax.experimental import pallas as pl
from jax.experimental.pallas import tpu as pltpu
from jax.sharding import Mesh
from jax.sharding import PartitionSpec as P

OCC = ("ylo", "x", "core")
VIR = ("z", "yhi")
F32 = jnp.float32
BF16 = jnp.bfloat16
I32 = jnp.int32


def iota(shape, dim):
    return lax.broadcasted_iota(I32, shape, dim)


def dot(a, b, da=1, db=0):
    return lax.dot_general(a, b, (((da,), (db,)), ((), ())), preferred_element_type=F32)


def encode(v):
    a = jnp.abs(v)
    small = a < 2.0**-60
    b = jnp.where(small, a * 2.0**60, a)
    e = jnp.floor(jnp.log2(jnp.maximum(b, 2.0**-70)))
    q = b * jnp.exp2(7.0 - e)
    up = q >= 255.5
    down = q < 127.5
    q = q * jnp.where(up, 0.5, jnp.where(down, 2.0, 1.0))
    e = e + jnp.where(up, 1.0, jnp.where(down, -1.0, 0.0)) - jnp.where(small, 60.0, 0.0)
    code = (e + 127.0) * 128.0 + (jnp.floor(q + 0.5) - 128.0)
    code = jnp.where(a < 2.0**-126, 0.0, code)
    return jnp.where(v < 0.0, -code, code).astype(I32)


def decode(c):
    c = c.astype(I32)
    m = jnp.abs(c)
    f = ((m & 127) + 128).astype(F32) * (1.0 / 128.0)
    v = f * jnp.exp2((m >> 7).astype(F32) - 127.0)
    v = jnp.where(m == 0, 0.0, v)
    return jnp.where(c < 0, -v, v).astype(BF16)


def prep_kernel(tile_k, kfirst, amps_ref, owners_ref, mask_ref, keep_ref, energy_ref, code_ref, slot_ref, meta_ref):
    k_width, rows = amps_ref.shape
    tiles, k_tiles = mask_ref.shape
    owners = meta_ref.shape[0]
    tile_rows = rows // tiles
    half = rows // 2
    own = owners_ref[...].astype(F32)
    i = iota((tiles, tiles), 0)
    j = iota((tiles, tiles), 1)
    own_row = jnp.sum(jnp.where(i == j, own, 0.0), axis=0, keepdims=True)
    earlier = jnp.where((own_row == own) & (j < i), 1.0, 0.0)
    before = jnp.where(own_row < own, 1.0, 0.0)
    k = jnp.sum(earlier, axis=1, keepdims=True)
    rank = jnp.sum(before, axis=1, keepdims=True) + k
    place = own * 2.0 + jnp.where(k >= 2.0, 1.0, 0.0)
    slot_ref[...] = jnp.sum(
        jnp.where(rank == j.astype(F32), place, 0.0), axis=0, keepdims=True
    ).astype(I32)
    lane = iota((tiles, 128), 1)
    keep = keep_ref[...].astype(F32)
    cols = jnp.where(
        lane == 0, rank, jnp.where(lane == 1, own, jnp.where(lane == 2, k, keep))
    ).astype(BF16)
    spread = jnp.where(iota((rows, tiles), 0) // tile_rows == iota((rows, tiles), 1), 1.0, 0.0).astype(BF16)
    per_row = dot(spread, cols)
    per_col = dot(cols, spread, 0, 1)
    column_tile = (kfirst[0] + iota((k_width, k_tiles), 0)) // tile_k
    select = jnp.where(column_tile == iota((k_width, k_tiles), 1), 1.0, 0.0).astype(BF16)
    present = dot(select, mask_ref[...].astype(F32).astype(BF16), 1, 1).astype(BF16)
    present = dot(present, spread, 1, 1)
    masked = jnp.where(present > 0.5, amps_ref[...].astype(F32), 0.0).astype(BF16)
    r = per_row[:, 0:1].astype(I32)
    target = (r % 2) * half + (r // 2) * tile_rows + iota((rows, 1), 0) % tile_rows
    moved = jnp.where(target == iota((rows, rows), 1), 1.0, 0.0).astype(BF16)
    code = encode(dot(masked, moved))
    code_ref[0] = code[:, :half].astype(jnp.int16)
    code_ref[1] = code[:, half:].astype(jnp.int16)
    energy = jnp.where(per_col[3:4] > 0.5, energy_ref[...].astype(F32), 0.0)
    to = per_col[1:2].astype(I32) * tile_rows + iota((1, rows), 1) % tile_rows
    big = iota((owners * tile_rows, rows), 0)
    sent = jnp.where(big == to, energy, 0.0).astype(BF16)
    position = jnp.where(per_row[:, 2:3].astype(I32) == iota((rows, 128), 1), 1.0, 0.0).astype(BF16)
    meta = dot(sent, position)
    start = jnp.sum(
        jnp.where(own_row < (iota((owners * tile_rows, tiles), 0) // tile_rows).astype(F32), 1.0, 0.0),
        axis=1,
        keepdims=True,
    ).astype(I32)
    odd = (start % 2).astype(F32)
    meta = jnp.where(iota(meta.shape, 1) == 4, odd, meta)
    meta_ref[...] = meta.astype(BF16).reshape(meta_ref.shape)


def prep(kfirst, tile_k, amps_t, owners, amp_mask, keep_mask, energy, owner_count):
    k_width, rows = amps_t.shape
    tile_rows = rows // amp_mask.shape[0]
    vmem = pl.BlockSpec(memory_space=pltpu.VMEM)

    def kernel(*refs):
        prep_kernel(tile_k, *refs)

    return pl.pallas_call(
        kernel,
        out_shape=(
            jax.ShapeDtypeStruct((2, k_width, rows // 2), jnp.int16),
            jax.ShapeDtypeStruct((1, amp_mask.shape[0]), I32),
            jax.ShapeDtypeStruct((owner_count, tile_rows, 128), BF16),
        ),
        in_specs=[pl.BlockSpec(memory_space=pltpu.SMEM)] + [vmem] * 5,
        out_specs=(vmem, vmem, vmem),
        compiler_params=pltpu.CompilerParams(vmem_limit_bytes=32 << 20),
        name="prep",
    )(kfirst, amps_t, owners, amp_mask, keep_mask, energy)


def place_tiles(slot, h, acc, out_ref):
    tile_rows = out_ref.shape[3]
    for n in range(acc.shape[0] // tile_rows):
        at = slot[0, 2 * n + h]
        out_ref[0, at // 2, at % 2] = acc[n * tile_rows : (n + 1) * tile_rows].astype(BF16)


def near_kernel(slot, where, code_ref, ints_ref, amps_ref, out_ref, acc_ref):
    step = pl.program_id(0)
    a = decode(code_ref[...]).T
    amps_ref[...] = a
    part = dot(a, ints_ref[...])

    @pl.when(step == 0)
    def _():
        acc_ref[...] = part

    @pl.when(step > 0)
    def _():
        acc_ref[...] += part

    @pl.when(step == pl.num_programs(0) - 1)
    def _():
        place_tiles(slot, where[0], acc_ref, out_ref)


def near(slot, where, code, ints, owner_count, tile_rows):
    depth, rows = code.shape
    width = ints.shape[1]
    steps = 4
    block = depth // steps
    return pl.pallas_call(
        near_kernel,
        out_shape=(
            jax.ShapeDtypeStruct((rows, depth), BF16),
            jax.ShapeDtypeStruct((2, owner_count, 2, tile_rows, width), BF16),
        ),
        grid_spec=pltpu.PrefetchScalarGridSpec(
            num_scalar_prefetch=2,
            grid=(steps,),
            in_specs=[
                pl.BlockSpec((block, rows), lambda s, *_: (s, 0)),
                pl.BlockSpec((block, width), lambda s, *_: (s, 0)),
            ],
            out_specs=(
                pl.BlockSpec((rows, block), lambda s, *_: (0, s)),
                pl.BlockSpec(
                    (1, owner_count, 2, tile_rows, width), lambda s, slot, where: (where[0], 0, 0, 0, 0)
                ),
            ),
            scratch_shapes=[pltpu.VMEM((rows, width), F32)],
        ),
        compiler_params=pltpu.CompilerParams(vmem_limit_bytes=40 << 20),
        cost_estimate=pl.CostEstimate(
            flops=2 * rows * depth * width, bytes_accessed=11 << 20, transcendentals=rows * depth
        ),
        name="near",
    )(slot, where, code, ints)


def far_kernel(slot, where, a0_ref, a1_ref, mine_ref, other_ref, _, out_ref):
    acc = dot(a0_ref[...], mine_ref[...]) + dot(a1_ref[...], other_ref[...])
    place_tiles(slot, where[0], acc, out_ref)


def far(slot, where, amps, mine, other, send):
    rows, depth = amps.shape
    width = mine.shape[1]
    owner_count, tile_rows = send.shape[1], send.shape[3]
    return pl.pallas_call(
        far_kernel,
        out_shape=jax.ShapeDtypeStruct(send.shape, BF16),
        grid_spec=pltpu.PrefetchScalarGridSpec(
            num_scalar_prefetch=2,
            grid=(1,),
            in_specs=[
                pl.BlockSpec((rows, depth // 2), lambda s, slot, where: (0, where[1])),
                pl.BlockSpec((rows, depth // 2), lambda s, slot, where: (0, 1 - where[1])),
                pl.BlockSpec(mine.shape, lambda s, *_: (0, 0)),
                pl.BlockSpec(mine.shape, lambda s, *_: (0, 0)),
                pl.BlockSpec(memory_space=pl.ANY),
            ],
            out_specs=pl.BlockSpec(
                (1, owner_count, 2, tile_rows, width), lambda s, slot, where: (1 - where[0], 0, 0, 0, 0)
            ),
        ),
        input_output_aliases={6: 0},
        compiler_params=pltpu.CompilerParams(vmem_limit_bytes=40 << 20),
        cost_estimate=pl.CostEstimate(
            flops=2 * rows * depth * width, bytes_accessed=8 << 20, transcendentals=0
        ),
        name="far",
    )(slot, where, amps, amps, mine, other, send)


def update_kernel(recv_ref, meta_ref, mix_ref, vir_ref, out_ref):
    meta = meta_ref[0].astype(F32)
    odd = meta[0:1, 4:5] > 0.5
    weight = mix_ref[0]
    energies = vir_ref[...]
    for k in range(4):
        energy = meta[:, k : k + 1]
        tile = jnp.where(odd, recv_ref[(k + 1) % 2, 0, k // 2].astype(F32), recv_ref[k % 2, 0, k // 2].astype(F32))
        tile = jnp.where(energy != 0.0, tile, 0.0).astype(BF16)
        out_ref[k] = (dot(weight, tile) / (energies - energy)).astype(BF16)


def update(recv, meta, mix, vir_energy):
    _, owner_count, two, tile_rows, width = recv.shape
    return pl.pallas_call(
        update_kernel,
        out_shape=jax.ShapeDtypeStruct((owner_count * 4, tile_rows, width), BF16),
        grid=(owner_count,),
        in_specs=[
            pl.BlockSpec((2, 1, two, tile_rows, width), lambda s: (0, s, 0, 0, 0)),
            pl.BlockSpec((1, tile_rows, 128), lambda s: (s, 0, 0)),
            pl.BlockSpec(mix.shape, lambda s: (0, 0, 0)),
            pl.BlockSpec((1, width), lambda s: (0, 0)),
        ],
        out_specs=pl.BlockSpec((4, tile_rows, width), lambda s: (s, 0, 0)),
        name="update",
    )(recv, meta, mix, vir_energy)


def shards(amps, ints, amp_mask, keep_mask, owners, occ_energy, vir_energy, mix):
    tiles_dev, k_tiles = amp_mask.shape
    rows, k_width = amps.shape
    tile_rows = rows // tiles_dev
    depth, width = ints.shape
    owner_count = lax.axis_size(OCC)
    h = lax.axis_index("yhi").astype(I32)
    c = lax.axis_index("core").astype(I32)
    kfirst = (lax.axis_index(VIR) * k_width).astype(I32).reshape(1)
    where = jnp.stack([h, c])
    code, slot, meta = prep(
        kfirst, depth // k_tiles, amps.T, owners, amp_mask, keep_mask, occ_energy.reshape(1, rows), owner_count
    )
    code = lax.all_to_all(code, "yhi", 0, 0, tiled=True)
    part = lax.dynamic_slice(ints, (c * (depth // 2), 0), (depth // 2, width))
    mine = lax.ppermute(part, ("ylo", "yhi"), [(n, 3 - n) for n in range(4)])
    other = lax.ppermute(mine, "core", [(0, 1), (1, 0)])
    meta = lax.all_to_all(meta, OCC, 0, 0, tiled=True)
    code = lax.all_gather(code.reshape(2 * k_width, rows // 2), "z", axis=0, tiled=True)
    decoded, send = near(slot, where, code, ints, owner_count, tile_rows)
    send = far(slot, where, decoded, mine, other, send)
    recv = lax.all_to_all(
        send.reshape(2 * owner_count, 2, tile_rows, width), ("yhi",) + OCC, 0, 0, tiled=True
    )
    recv = recv.reshape(2, owner_count, 2, tile_rows, width)
    return update(recv, meta, mix, vir_energy.reshape(1, width))


def solution(mesh):
    split = Mesh(mesh.devices.reshape(2, 4, 2, 16, 2), OCC + VIR)
    in_specs = (
        P(OCC, VIR),
        P(None, VIR),
        P(OCC, None),
        P(OCC, VIR),
        P(OCC, None),
        P(OCC),
        P(VIR),
        P(OCC, None, None),
    )
    return jax.shard_map(
        shards, mesh=split, in_specs=in_specs, out_specs=P(OCC, None, VIR), check_vma=False
    )
```

```python
import jax
import jax.numpy as jnp
from jax import lax
from jax.experimental import pallas as pl
from jax.experimental.pallas import tpu as pltpu
from jax.sharding import Mesh
from jax.sharding import PartitionSpec as P

OCC = ("ylo", "x", "core")
VIR = ("z", "yhi")
F32 = jnp.float32
BF16 = jnp.bfloat16
I32 = jnp.int32


def iota(shape, dim):
    return lax.broadcasted_iota(I32, shape, dim)


def dot(a, b, da=1, db=0):
    return lax.dot_general(a, b, (((da,), (db,)), ((), ())), preferred_element_type=F32)


def encode(v):
    a = jnp.abs(v)
    small = a < 2.0**-60
    b = jnp.where(small, a * 2.0**60, a)
    e = jnp.floor(jnp.log2(jnp.maximum(b, 2.0**-70)))
    q = b * jnp.exp2(7.0 - e)
    up = q >= 255.5
    down = q < 127.5
    q = q * jnp.where(up, 0.5, jnp.where(down, 2.0, 1.0))
    e = e + jnp.where(up, 1.0, jnp.where(down, -1.0, 0.0)) - jnp.where(small, 60.0, 0.0)
    code = (e + 127.0) * 128.0 + (jnp.floor(q + 0.5) - 128.0)
    code = jnp.where(a < 2.0**-126, 0.0, code)
    return jnp.where(v < 0.0, -code, code).astype(I32)


def decode(c):
    c = c.astype(I32)
    m = jnp.abs(c)
    v = ((m & 127) | 128).astype(F32) * jnp.exp2((m >> 7).astype(F32) - 127.0)
    v = jnp.where(m == 0, 0.0, v)
    return jnp.where(c < 0, -v, v).astype(BF16)


def prep_kernel(
    tile_k, where, amps_ref, owners_ref, mask_ref, keep_ref, energy_ref, ints_ref, code_ref, slot_ref, meta_ref, part_ref, sem
):
    half_depth = part_ref.shape[0]
    first = pl.multiple_of(where[1] * half_depth, half_depth)
    copy = pltpu.make_async_copy(ints_ref.at[pl.ds(first, half_depth)], part_ref, sem)
    copy.start()
    k_width, rows = amps_ref.shape
    tiles, k_tiles = mask_ref.shape
    owners = meta_ref.shape[0]
    tile_rows = rows // tiles
    half = rows // 2
    own = owners_ref[...].astype(F32)
    i = iota((tiles, tiles), 0)
    j = iota((tiles, tiles), 1)
    own_row = jnp.sum(jnp.where(i == j, own, 0.0), axis=0, keepdims=True)
    earlier = jnp.where((own_row == own) & (j < i), 1.0, 0.0)
    before = jnp.where(own_row < own, 1.0, 0.0)
    k = jnp.sum(earlier, axis=1, keepdims=True)
    rank = jnp.sum(before, axis=1, keepdims=True) + k
    place = own * 2.0 + jnp.where(k >= 2.0, 1.0, 0.0)
    slot_ref[...] = jnp.sum(
        jnp.where(rank == j.astype(F32), place, 0.0), axis=0, keepdims=True
    ).astype(I32)
    lane = iota((tiles, 128), 1)
    keep = keep_ref[...].astype(F32)
    cols = jnp.where(
        lane == 0, rank, jnp.where(lane == 1, own, jnp.where(lane == 2, k, keep))
    ).astype(BF16)
    spread = jnp.where(iota((rows, tiles), 0) // tile_rows == iota((rows, tiles), 1), 1.0, 0.0).astype(BF16)
    per_row = dot(spread, cols)
    per_col = dot(cols, spread, 0, 1)
    column_tile = (where[2] + iota((k_width, k_tiles), 0)) // tile_k
    select = jnp.where(column_tile == iota((k_width, k_tiles), 1), 1.0, 0.0).astype(BF16)
    present = dot(select, mask_ref[...].astype(F32).astype(BF16), 1, 1).astype(BF16)
    present = dot(present, spread, 1, 1)
    masked = jnp.where(present > 0.5, amps_ref[...].astype(F32), 0.0).astype(BF16)
    r = per_row[:, 0:1].astype(I32)
    target = (r % 2) * half + (r // 2) * tile_rows + iota((rows, 1), 0) % tile_rows
    moved = jnp.where(target == iota((rows, rows), 1), 1.0, 0.0).astype(BF16)
    code = encode(dot(masked, moved))
    code_ref[0] = code[:, :half].astype(jnp.int16)
    code_ref[1] = code[:, half:].astype(jnp.int16)
    energy = jnp.where(per_col[3:4] > 0.5, energy_ref[...].astype(F32), 0.0)
    to = per_col[1:2].astype(I32) * tile_rows + iota((1, rows), 1) % tile_rows
    big = iota((owners * tile_rows, rows), 0)
    sent = jnp.where(big == to, energy, 0.0).astype(BF16)
    position = jnp.where(per_row[:, 2:3].astype(I32) == iota((rows, 128), 1), 1.0, 0.0).astype(BF16)
    meta = dot(sent, position)
    start = jnp.sum(
        jnp.where(own_row < (iota((owners * tile_rows, tiles), 0) // tile_rows).astype(F32), 1.0, 0.0),
        axis=1,
        keepdims=True,
    ).astype(I32)
    odd = (start % 2).astype(F32)
    meta = jnp.where(iota(meta.shape, 1) == 4, odd, meta)
    meta_ref[...] = meta.astype(BF16).reshape(meta_ref.shape)
    copy.wait()


def prep(where, amps_t, owners, amp_mask, keep_mask, energy, ints, owner_count):
    tile_k = ints.shape[0] // amp_mask.shape[1]
    k_width, rows = amps_t.shape
    tile_rows = rows // amp_mask.shape[0]
    vmem = pl.BlockSpec(memory_space=pltpu.VMEM)

    def kernel(*refs):
        prep_kernel(tile_k, *refs)

    return pl.pallas_call(
        kernel,
        out_shape=(
            jax.ShapeDtypeStruct((2, k_width, rows // 2), jnp.int16),
            jax.ShapeDtypeStruct((1, amp_mask.shape[0]), I32),
            jax.ShapeDtypeStruct((owner_count, tile_rows, 128), BF16),
            jax.ShapeDtypeStruct((ints.shape[0] // 2, ints.shape[1]), BF16),
        ),
        in_specs=[pl.BlockSpec(memory_space=pltpu.SMEM)] + [vmem] * 5 + [pl.BlockSpec(memory_space=pltpu.HBM)],
        out_specs=(vmem, vmem, vmem, pl.BlockSpec(memory_space=pltpu.HBM)),
        scratch_shapes=[pltpu.SemaphoreType.DMA],
        compiler_params=pltpu.CompilerParams(vmem_limit_bytes=62 << 20),
        name="prep",
    )(where, amps_t, owners, amp_mask, keep_mask, energy, ints)


def place_tiles(slot, h, acc, out_ref):
    tile_rows = out_ref.shape[3]
    for n in range(acc.shape[0] // tile_rows):
        at = slot[0, 2 * n + h]
        out_ref[0, at // 2, at % 2] = (acc[n * tile_rows : (n + 1) * tile_rows] * (1.0 / 128.0)).astype(BF16)


def near_kernel(slot, where, code_ref, ints_ref, amps_ref, out_ref, acc_ref):
    step = pl.program_id(0)
    a = decode(code_ref[...]).T
    amps_ref[...] = a
    part = dot(a, ints_ref[...])

    @pl.when(step == 0)
    def _():
        acc_ref[...] = part

    @pl.when(step > 0)
    def _():
        acc_ref[...] += part

    @pl.when(step == pl.num_programs(0) - 1)
    def _():
        place_tiles(slot, where[0], acc_ref, out_ref)


def near(slot, where, code, ints, owner_count, tile_rows):
    depth, rows = code.shape
    width = ints.shape[1]
    steps = 4
    block = depth // steps
    return pl.pallas_call(
        near_kernel,
        out_shape=(
            jax.ShapeDtypeStruct((rows, depth), BF16),
            jax.ShapeDtypeStruct((2, owner_count, 2, tile_rows, width), BF16),
        ),
        grid_spec=pltpu.PrefetchScalarGridSpec(
            num_scalar_prefetch=2,
            grid=(steps,),
            in_specs=[
                pl.BlockSpec((block, rows), lambda s, *_: (s, 0)),
                pl.BlockSpec((block, width), lambda s, *_: (s, 0)),
            ],
            out_specs=(
                pl.BlockSpec((rows, block), lambda s, *_: (0, s)),
                pl.BlockSpec(
                    (1, owner_count, 2, tile_rows, width), lambda s, slot, where: (where[0], 0, 0, 0, 0)
                ),
            ),
            scratch_shapes=[pltpu.VMEM((rows, width), F32)],
        ),
        compiler_params=pltpu.CompilerParams(vmem_limit_bytes=58 << 20),
        cost_estimate=pl.CostEstimate(
            flops=2 * rows * depth * width, bytes_accessed=11 << 20, transcendentals=rows * depth
        ),
        name="near",
    )(slot, where, code, ints)


def far_kernel(slot, where, amps_ref, mine_ref, other_ref, _, out_ref, acc_ref):
    step = pl.program_id(0)
    last = pl.num_programs(0) - 1

    @pl.when(step == 0)
    def _():
        acc_ref[...] = dot(amps_ref[...], mine_ref[...])

    @pl.when((step > 0) & (step < 2))
    def _():
        acc_ref[...] += dot(amps_ref[...], mine_ref[...])

    @pl.when(step >= 2)
    def _():
        acc_ref[...] += dot(amps_ref[...], other_ref[...])

    @pl.when(step == last)
    def _():
        place_tiles(slot, where[0], acc_ref, out_ref)


def far(slot, where, amps, mine, other, send):
    rows, depth = amps.shape
    width = mine.shape[1]
    owner_count, tile_rows = send.shape[1], send.shape[3]
    block = depth // 4
    return pl.pallas_call(
        far_kernel,
        out_shape=jax.ShapeDtypeStruct(send.shape, BF16),
        grid_spec=pltpu.PrefetchScalarGridSpec(
            num_scalar_prefetch=2,
            grid=(4,),
            in_specs=[
                pl.BlockSpec(
                    (rows, block),
                    lambda s, slot, where: (0, jnp.where(s < 2, where[1], 1 - where[1]) * 2 + s % 2),
                ),
                pl.BlockSpec((block, width), lambda s, *_: (jnp.minimum(s, 1), 0)),
                pl.BlockSpec((block, width), lambda s, *_: (jnp.maximum(s - 2, 0), 0)),
                pl.BlockSpec(memory_space=pl.ANY),
            ],
            out_specs=pl.BlockSpec(
                (1, owner_count, 2, tile_rows, width), lambda s, slot, where: (1 - where[0], 0, 0, 0, 0)
            ),
            scratch_shapes=[pltpu.VMEM((rows, width), F32)],
        ),
        input_output_aliases={5: 0},
        compiler_params=pltpu.CompilerParams(vmem_limit_bytes=50 << 20),
        cost_estimate=pl.CostEstimate(
            flops=2 * rows * depth * width, bytes_accessed=8 << 20, transcendentals=0
        ),
        name="far",
    )(slot, where, amps, mine, other, send)


def update_kernel(recv_ref, meta_ref, mix_ref, vir_ref, out_ref, weight_ref):
    tile_rows = mix_ref.shape[1]
    tall = weight_ref.shape[0]
    batch = meta_ref.shape[0]

    @pl.when(pl.program_id(0) == 0)
    def _():
        copies = jnp.where(iota((tall, tile_rows), 0) % tile_rows == iota((tall, tile_rows), 1), 1.0, 0.0).astype(BF16)
        wide = dot(dot(copies, mix_ref[0]).astype(BF16), copies, 1, 1)
        same = iota((tall, tall), 0) // tile_rows == iota((tall, tall), 1) // tile_rows
        weight_ref[...] = jnp.where(same, wide, 0.0).astype(BF16)

    tiles, energies = [], []
    for s in range(batch):
        meta = meta_ref[s].astype(F32)
        odd = meta[0:1, 4:5] > 0.5
        for k in range(4):
            energy = meta[:, k : k + 1]
            tile = jnp.where(odd, recv_ref[(k + 1) % 2, s, k // 2].astype(F32), recv_ref[k % 2, s, k // 2].astype(F32))
            tiles.append(jnp.where(energy != 0.0, tile, 0.0).astype(BF16))
            energies.append(energy)
    mixed = dot(weight_ref[...], jnp.concatenate(tiles, axis=0))
    new = mixed / (vir_ref[...] - jnp.concatenate(energies, axis=0))
    out_ref[...] = new.astype(BF16).reshape(out_ref.shape)


def update(recv, meta, mix, vir_energy):
    _, owner_count, two, tile_rows, width = recv.shape
    batch = 2
    return pl.pallas_call(
        update_kernel,
        out_shape=jax.ShapeDtypeStruct((owner_count * 4, tile_rows, width), BF16),
        grid=(owner_count // batch,),
        in_specs=[
            pl.BlockSpec((2, batch, two, tile_rows, width), lambda s: (0, s, 0, 0, 0)),
            pl.BlockSpec((batch, tile_rows, 128), lambda s: (s, 0, 0)),
            pl.BlockSpec(mix.shape, lambda s: (0, 0, 0)),
            pl.BlockSpec((1, width), lambda s: (0, 0)),
        ],
        out_specs=pl.BlockSpec((batch * 4, tile_rows, width), lambda s: (s, 0, 0)),
        scratch_shapes=[pltpu.VMEM((batch * 4 * tile_rows, batch * 4 * tile_rows), BF16)],
        name="update",
    )(recv, meta, mix, vir_energy)


def shards(amps, ints, amp_mask, keep_mask, owners, occ_energy, vir_energy, mix):
    tiles_dev, k_tiles = amp_mask.shape
    rows, k_width = amps.shape
    tile_rows = rows // tiles_dev
    depth, width = ints.shape
    owner_count = lax.axis_size(OCC)
    h = lax.axis_index("yhi").astype(I32)
    c = lax.axis_index("core").astype(I32)
    kfirst = (lax.axis_index(VIR) * k_width).astype(I32)
    where = jnp.stack([h, c, kfirst])
    code, slot, meta, part = prep(
        where, amps.T, owners, amp_mask, keep_mask, occ_energy.reshape(1, rows), ints, owner_count
    )
    code = lax.all_to_all(code, "yhi", 0, 0, tiled=True)
    meta = lax.all_to_all(meta, OCC, 0, 0, tiled=True)
    mine = lax.ppermute(part, ("ylo", "yhi"), [(n, 3 - n) for n in range(4)])
    code = lax.all_gather(code.reshape(2 * k_width, rows // 2), "z", axis=0, tiled=True)
    mine, code = lax.optimization_barrier((mine, code))
    other = lax.ppermute(mine, "core", [(0, 1), (1, 0)])
    decoded, send = near(slot, where, code, ints, owner_count, tile_rows)
    send = far(slot, where, decoded, mine, other, send)
    recv = lax.all_to_all(
        send.reshape(2 * owner_count, 2, tile_rows, width), ("yhi",) + OCC, 0, 0, tiled=True
    )
    recv = recv.reshape(2, owner_count, 2, tile_rows, width)
    return update(recv, meta, mix, vir_energy.reshape(1, width))


def solution(mesh):
    split = Mesh(mesh.devices.reshape(2, 4, 2, 16, 2), OCC + VIR)
    in_specs = (
        P(OCC, VIR),
        P(None, VIR),
        P(OCC, None),
        P(OCC, VIR),
        P(OCC, None),
        P(OCC),
        P(VIR),
        P(OCC, None, None),
    )
    return jax.shard_map(
        shards, mesh=split, in_specs=in_specs, out_specs=P(OCC, None, VIR), check_vma=False
    )
```

```python
import jax
import jax.numpy as jnp
from jax import lax
from jax.experimental import pallas as pl
from jax.experimental.pallas import tpu as pltpu
from jax.sharding import Mesh
from jax.sharding import PartitionSpec as P

OCC = ("ylo", "x", "core")
VIR = ("z", "yhi")
F32 = jnp.float32
BF16 = jnp.bfloat16
I32 = jnp.int32
NEAR_LIMIT = 32
FAR_LIMIT = 32


def iota(shape, dim):
    return lax.broadcasted_iota(I32, shape, dim)


def dot(a, b, da=1, db=0):
    return lax.dot_general(a, b, (((da,), (db,)), ((), ())), preferred_element_type=F32)


def encode(v):
    a = jnp.abs(v)
    small = a < 2.0**-60
    b = jnp.where(small, a * 2.0**60, a)
    e = jnp.floor(jnp.log2(jnp.maximum(b, 2.0**-70)))
    q = b * jnp.exp2(7.0 - e)
    up = q >= 255.5
    down = q < 127.5
    q = q * jnp.where(up, 0.5, jnp.where(down, 2.0, 1.0))
    e = e + jnp.where(up, 1.0, jnp.where(down, -1.0, 0.0)) - jnp.where(small, 60.0, 0.0)
    code = (e + 127.0) * 128.0 + (jnp.floor(q + 0.5) - 128.0)
    code = jnp.where(a < 2.0**-126, 0.0, code)
    return jnp.where(v < 0.0, -code, code).astype(I32)


def decode(c):
    c = c.astype(I32)
    m = jnp.abs(c)
    v = ((m & 127) | 128).astype(F32) * jnp.exp2((m >> 7).astype(F32) - 127.0)
    v = jnp.where(m == 0, 0.0, v)
    return jnp.where(c < 0, -v, v).astype(BF16)


def prep_kernel(
    tile_k, where, amps_ref, owners_ref, mask_ref, keep_ref, energy_ref, code_ref, slot_ref, meta_ref
):
    k_width, rows = amps_ref.shape
    tiles, k_tiles = mask_ref.shape
    owners = meta_ref.shape[0]
    tile_rows = rows // tiles
    half = rows // 2
    own = owners_ref[...].astype(F32)
    i = iota((tiles, tiles), 0)
    j = iota((tiles, tiles), 1)
    own_row = jnp.sum(jnp.where(i == j, own, 0.0), axis=0, keepdims=True)
    earlier = jnp.where((own_row == own) & (j < i), 1.0, 0.0)
    before = jnp.where(own_row < own, 1.0, 0.0)
    k = jnp.sum(earlier, axis=1, keepdims=True)
    rank = jnp.sum(before, axis=1, keepdims=True) + k
    place = own * 2.0 + jnp.where(k >= 2.0, 1.0, 0.0)
    slot_ref[...] = jnp.sum(
        jnp.where(rank == j.astype(F32), place, 0.0), axis=0, keepdims=True
    ).astype(I32)
    lane = iota((tiles, 128), 1)
    keep = keep_ref[...].astype(F32)
    cols = jnp.where(
        lane == 0, rank, jnp.where(lane == 1, own, jnp.where(lane == 2, k, keep))
    ).astype(BF16)
    spread = jnp.where(iota((rows, tiles), 0) // tile_rows == iota((rows, tiles), 1), 1.0, 0.0).astype(BF16)
    per_row = dot(spread, cols)
    per_col = dot(cols, spread, 0, 1)
    column_tile = (where[2] + iota((k_width, k_tiles), 0)) // tile_k
    select = jnp.where(column_tile == iota((k_width, k_tiles), 1), 1.0, 0.0).astype(BF16)
    present = dot(select, mask_ref[...].astype(F32).astype(BF16), 1, 1).astype(BF16)
    present = dot(present, spread, 1, 1)
    masked = jnp.where(present > 0.5, amps_ref[...].astype(F32), 0.0).astype(BF16)
    r = per_row[:, 0:1].astype(I32)
    target = (r % 2) * half + (r // 2) * tile_rows + iota((rows, 1), 0) % tile_rows
    moved = jnp.where(target == iota((rows, rows), 1), 1.0, 0.0).astype(BF16)
    code = encode(dot(masked, moved))
    code_ref[0] = code[:, :half].astype(jnp.int16)
    code_ref[1] = code[:, half:].astype(jnp.int16)
    energy = jnp.where(per_col[3:4] > 0.5, energy_ref[...].astype(F32), 0.0)
    to = per_col[1:2].astype(I32) * tile_rows + iota((1, rows), 1) % tile_rows
    big = iota((owners * tile_rows, rows), 0)
    sent = jnp.where(big == to, energy, 0.0).astype(BF16)
    position = jnp.where(per_row[:, 2:3].astype(I32) == iota((rows, 128), 1), 1.0, 0.0).astype(BF16)
    meta = dot(sent, position)
    start = jnp.sum(
        jnp.where(own_row < (iota((owners * tile_rows, tiles), 0) // tile_rows).astype(F32), 1.0, 0.0),
        axis=1,
        keepdims=True,
    ).astype(I32)
    odd = (start % 2).astype(F32)
    meta = jnp.where(iota(meta.shape, 1) == 4, odd, meta)
    meta_ref[...] = meta.astype(BF16).reshape(meta_ref.shape)


def prep(where, amps_t, owners, amp_mask, keep_mask, energy, tile_k, owner_count):
    k_width, rows = amps_t.shape
    tile_rows = rows // amp_mask.shape[0]
    vmem = pl.BlockSpec(memory_space=pltpu.VMEM)

    def kernel(*refs):
        prep_kernel(tile_k, *refs)

    return pl.pallas_call(
        kernel,
        out_shape=(
            jax.ShapeDtypeStruct((2, k_width, rows // 2), jnp.int16),
            jax.ShapeDtypeStruct((1, amp_mask.shape[0]), I32),
            jax.ShapeDtypeStruct((owner_count, tile_rows, 128), BF16),
        ),
        in_specs=[pl.BlockSpec(memory_space=pltpu.SMEM)] + [vmem] * 5,
        out_specs=(vmem, vmem, vmem),
        compiler_params=pltpu.CompilerParams(vmem_limit_bytes=24 << 20),
        name="prep",
    )(where, amps_t, owners, amp_mask, keep_mask, energy)


def place_tiles(slot, h, first, acc, out_ref, to):
    tile_rows = out_ref.shape[3]
    for n in range(acc.shape[0] // tile_rows):
        at = slot[0, 2 * (first + n) + h]
        tile = acc[n * tile_rows : (n + 1) * tile_rows] * (1.0 / 128.0)
        out_ref[to, at // 2, at % 2] = tile.astype(BF16)


def near_kernel(slot, where, code_ref, ints_ref, amps_ref, out_ref):
    depth, rows = code_ref.shape
    block = depth // 8
    for k in range(0, depth, block):
        amps_ref[:, k : k + block] = decode(code_ref[k : k + block]).T
    tall = rows // 4
    for r in range(0, rows, tall):
        acc = dot(amps_ref[r : r + tall], ints_ref[...])
        place_tiles(slot, where[0], r // out_ref.shape[3], acc, out_ref, where[0])


def near(slot, where, code, ints, owner_count, tile_rows):
    depth, rows = code.shape
    width = ints.shape[1]
    smem = pl.BlockSpec(memory_space=pltpu.SMEM)
    vmem = pl.BlockSpec(memory_space=pltpu.VMEM)
    return pl.pallas_call(
        near_kernel,
        out_shape=(
            jax.ShapeDtypeStruct((rows, depth), BF16),
            jax.ShapeDtypeStruct((2, owner_count, 2, tile_rows, width), BF16),
        ),
        in_specs=[smem, smem, vmem, vmem],
        out_specs=(vmem, vmem),
        compiler_params=pltpu.CompilerParams(vmem_limit_bytes=NEAR_LIMIT << 20),
        cost_estimate=pl.CostEstimate(
            flops=2 * rows * depth * width, bytes_accessed=11 << 20, transcendentals=rows * depth
        ),
        name="near",
    )(slot, where, code, ints)


def far_kernel(slot, where, amps_ref, mine_ref, other_ref, _, out_ref):
    rows = amps_ref.shape[0]
    half = mine_ref.shape[0]
    c = where[1]
    first = pl.multiple_of(c * half, half)
    second = pl.multiple_of((1 - c) * half, half)
    tall = rows // 4
    for r in range(0, rows, tall):
        acc = dot(amps_ref[r : r + tall, pl.ds(first, half)], mine_ref[...])
        acc += dot(amps_ref[r : r + tall, pl.ds(second, half)], other_ref[...])
        place_tiles(slot, where[0], r // out_ref.shape[3], acc, out_ref, 1 - where[0])


def far(slot, where, amps, mine, other, send):
    rows, depth = amps.shape
    width = mine.shape[1]
    smem = pl.BlockSpec(memory_space=pltpu.SMEM)
    vmem = pl.BlockSpec(memory_space=pltpu.VMEM)
    return pl.pallas_call(
        far_kernel,
        out_shape=jax.ShapeDtypeStruct(send.shape, BF16),
        in_specs=[smem, smem, vmem, vmem, vmem, vmem],
        out_specs=vmem,
        input_output_aliases={5: 0},
        compiler_params=pltpu.CompilerParams(vmem_limit_bytes=FAR_LIMIT << 20),
        cost_estimate=pl.CostEstimate(
            flops=2 * rows * depth * width, bytes_accessed=8 << 20, transcendentals=0
        ),
        name="far",
    )(slot, where, amps, mine, other, send)


def update_kernel(recv_ref, meta_ref, mix_ref, vir_ref, out_ref, weight_ref, new_ref, sems):
    tile_rows = mix_ref.shape[1]
    tall = weight_ref.shape[0]
    batch = tall // (4 * tile_rows)
    copies = jnp.where(iota((tall, tile_rows), 0) % tile_rows == iota((tall, tile_rows), 1), 1.0, 0.0).astype(BF16)
    wide = dot(dot(copies, mix_ref[0]).astype(BF16), copies, 1, 1)
    same = iota((tall, tall), 0) // tile_rows == iota((tall, tall), 1) // tile_rows
    weight_ref[...] = jnp.where(same, wide, 0.0).astype(BF16)
    writes = []
    for step in range(meta_ref.shape[0] // batch):
        tiles, energies = [], []
        for s in range(step * batch, (step + 1) * batch):
            meta = meta_ref[s].astype(F32)
            odd = meta[0:1, 4:5] > 0.5
            for k in range(4):
                energy = meta[:, k : k + 1]
                even_tile = recv_ref[k % 2, s, k // 2].astype(F32)
                odd_tile = recv_ref[(k + 1) % 2, s, k // 2].astype(F32)
                tile = jnp.where(odd, odd_tile, even_tile)
                tiles.append(jnp.where(energy != 0.0, tile, 0.0).astype(BF16))
                energies.append(energy)
        mixed = dot(weight_ref[...], jnp.concatenate(tiles, axis=0))
        new = mixed / (vir_ref[...] - jnp.concatenate(energies, axis=0))
        at = pl.ds(step * batch * 4, batch * 4)
        new_ref[at] = new.astype(BF16).reshape((batch * 4,) + new_ref.shape[1:])
        write = pltpu.make_async_copy(new_ref.at[at], out_ref.at[at], sems.at[step])
        write.start()
        writes.append(write)
    for write in writes:
        write.wait()


def update(recv, meta, mix, vir_energy):
    _, owner_count, two, tile_rows, width = recv.shape
    batch = 2
    vmem = pl.BlockSpec(memory_space=pltpu.VMEM)
    return pl.pallas_call(
        update_kernel,
        out_shape=jax.ShapeDtypeStruct((owner_count * 4, tile_rows, width), BF16),
        in_specs=[vmem] * 4,
        out_specs=pl.BlockSpec(memory_space=pl.ANY),
        scratch_shapes=[
            pltpu.VMEM((batch * 4 * tile_rows, batch * 4 * tile_rows), BF16),
            pltpu.VMEM((owner_count * 4, tile_rows, width), BF16),
            pltpu.SemaphoreType.DMA((owner_count // batch,)),
        ],
        compiler_params=pltpu.CompilerParams(vmem_limit_bytes=24 << 20),
        name="update",
    )(recv, meta, mix, vir_energy)


def shards(amps, ints, amp_mask, keep_mask, owners, occ_energy, vir_energy, mix):
    tiles_dev, k_tiles = amp_mask.shape
    rows, k_width = amps.shape
    tile_rows = rows // tiles_dev
    depth, width = ints.shape
    owner_count = lax.axis_size(OCC)
    h = lax.axis_index("yhi").astype(I32)
    c = lax.axis_index("core").astype(I32)
    kfirst = (lax.axis_index(VIR) * k_width).astype(I32)
    where = jnp.stack([h, c, kfirst])
    code, slot, meta = prep(
        where, amps.T, owners, amp_mask, keep_mask, occ_energy.reshape(1, rows), depth // k_tiles, owner_count
    )
    code, meta, ints_late = lax.optimization_barrier((code, meta, ints))
    code = lax.all_to_all(code, "yhi", 0, 0, tiled=True)
    meta = lax.all_to_all(meta, OCC, 0, 0, tiled=True)
    part = lax.dynamic_slice(ints_late, (c * (depth // 2), 0), (depth // 2, width))
    mine = lax.ppermute(part, ("ylo", "yhi"), [(n, 3 - n) for n in range(4)])
    code, meta = lax.optimization_barrier((code, meta))
    code = lax.all_gather(code.reshape(2 * k_width, rows // 2), "z", axis=0, tiled=True)
    mine, code = lax.optimization_barrier((mine, code))
    other = lax.ppermute(mine, "core", [(0, 1), (1, 0)])
    decoded, send = near(slot, where, code, ints, owner_count, tile_rows)
    send = far(slot, where, decoded, mine, other, send)
    recv = lax.all_to_all(
        send.reshape(2 * owner_count, 2, tile_rows, width), ("yhi",) + OCC, 0, 0, tiled=True
    )
    recv = recv.reshape(2, owner_count, 2, tile_rows, width)
    return update(recv, meta, mix, vir_energy.reshape(1, width))


def solution(mesh):
    split = Mesh(mesh.devices.reshape(2, 4, 2, 16, 2), OCC + VIR)
    in_specs = (
        P(OCC, VIR),
        P(None, VIR),
        P(OCC, None),
        P(OCC, VIR),
        P(OCC, None),
        P(OCC),
        P(VIR),
        P(OCC, None, None),
    )
    return jax.shard_map(
        shards, mesh=split, in_specs=in_specs, out_specs=P(OCC, None, VIR), check_vma=False
    )
```

```python
import jax
import jax.numpy as jnp
from jax import lax
from jax.experimental import pallas as pl
from jax.experimental.pallas import tpu as pltpu
from jax.sharding import Mesh
from jax.sharding import PartitionSpec as P

OCC = ("ylo", "x", "core")
VIR = ("z", "yhi")
F32 = jnp.float32
BF16 = jnp.bfloat16
I32 = jnp.int32
NEAR_LIMIT = 32
FAR_LIMIT = 32


def iota(shape, dim):
    return lax.broadcasted_iota(I32, shape, dim)


def dot(a, b, da=1, db=0):
    return lax.dot_general(a, b, (((da,), (db,)), ((), ())), preferred_element_type=F32)


def encode(v):
    a = jnp.abs(v)
    small = a < 2.0**-60
    b = jnp.where(small, a * 2.0**60, a)
    e = jnp.floor(jnp.log2(jnp.maximum(b, 2.0**-70)))
    q = b * jnp.exp2(7.0 - e)
    up = q >= 255.5
    down = q < 127.5
    q = q * jnp.where(up, 0.5, jnp.where(down, 2.0, 1.0))
    e = e + jnp.where(up, 1.0, jnp.where(down, -1.0, 0.0)) - jnp.where(small, 60.0, 0.0)
    code = (e + 127.0) * 128.0 + (jnp.floor(q + 0.5) - 128.0)
    code = jnp.where(a < 2.0**-126, 0.0, code)
    return jnp.where(v < 0.0, -code, code).astype(I32)


def decode(c):
    c = c.astype(I32)
    m = jnp.abs(c)
    v = ((m & 127) | 128).astype(F32) * jnp.exp2((m >> 7).astype(F32) - 127.0)
    v = jnp.where(m == 0, 0.0, v)
    return jnp.where(c < 0, -v, v).astype(BF16)


def prep_kernel(
    tile_k, where, amps_ref, owners_ref, mask_ref, keep_ref, energy_ref, code_ref, slot_ref, meta_ref
):
    k_width, rows = amps_ref.shape
    k_tiles, tiles = mask_ref.shape
    owners = meta_ref.shape[0]
    tile_rows = rows // tiles
    half = rows // 2
    own_row = owners_ref[...].astype(F32)
    i = iota((tiles, tiles), 0)
    j = iota((tiles, tiles), 1)
    own = jnp.sum(jnp.where(i == j, own_row, 0.0), axis=1, keepdims=True)
    earlier = jnp.where((own_row == own) & (j < i), 1.0, 0.0)
    before = jnp.where(own_row < own, 1.0, 0.0)
    k = jnp.sum(earlier, axis=1, keepdims=True)
    rank = jnp.sum(before, axis=1, keepdims=True) + k
    place = own * 2.0 + jnp.where(k >= 2.0, 1.0, 0.0)
    slot_ref[...] = jnp.sum(
        jnp.where(rank == j.astype(F32), place, 0.0), axis=0, keepdims=True
    ).astype(I32)
    lane = iota((tiles, 128), 1)
    keep = jnp.sum(jnp.where(i == j, keep_ref[...].astype(F32), 0.0), axis=1, keepdims=True)
    cols = jnp.where(
        lane == 0, rank, jnp.where(lane == 1, own, jnp.where(lane == 2, k, keep))
    ).astype(BF16)
    spread = jnp.where(iota((rows, tiles), 0) // tile_rows == iota((rows, tiles), 1), 1.0, 0.0).astype(BF16)
    per_row = dot(spread, cols)
    per_col = dot(cols, spread, 0, 1)
    column_tile = (where[2] + iota((k_width, k_tiles), 0)) // tile_k
    select = jnp.where(column_tile == iota((k_width, k_tiles), 1), 1.0, 0.0).astype(BF16)
    present = dot(select, mask_ref[...].astype(F32).astype(BF16)).astype(BF16)
    present = dot(present, spread, 1, 1)
    masked = jnp.where(present > 0.5, amps_ref[...].astype(F32), 0.0).astype(BF16)
    r = per_row[:, 0:1].astype(I32)
    target = ((r + where[0]) % 2) * half + (r // 2) * tile_rows + iota((rows, 1), 0) % tile_rows
    moved = jnp.where(target == iota((rows, rows), 1), 1.0, 0.0).astype(BF16)
    code = encode(dot(masked, moved))
    code_ref[0] = code[:, :half].astype(jnp.int16)
    code_ref[1] = code[:, half:].astype(jnp.int16)
    energy = energy_ref[...].astype(F32)
    energy = jnp.concatenate([energy[n : n + 1] for n in range(energy.shape[0])], axis=1)
    energy = jnp.where(per_col[3:4] > 0.5, energy, 0.0)
    to = per_col[1:2].astype(I32) * tile_rows + iota((1, rows), 1) % tile_rows
    big = iota((owners * tile_rows, rows), 0)
    sent = jnp.where(big == to, energy, 0.0).astype(BF16)
    position = jnp.where(per_row[:, 2:3].astype(I32) == iota((rows, 128), 1), 1.0, 0.0).astype(BF16)
    meta = dot(sent, position)
    start = jnp.sum(
        jnp.where(own_row < (iota((owners * tile_rows, tiles), 0) // tile_rows).astype(F32), 1.0, 0.0),
        axis=1,
        keepdims=True,
    ).astype(I32)
    odd = (start % 2).astype(F32)
    meta = jnp.where(iota(meta.shape, 1) == 4, odd, meta)
    meta_ref[...] = meta.astype(BF16).reshape(meta_ref.shape)


def prep(where, amps_t, owners, amp_mask, keep_mask, energy, tile_k, owner_count):
    k_width, rows = amps_t.shape
    tiles = amp_mask.shape[1]
    tile_rows = rows // tiles
    vmem = pl.BlockSpec(memory_space=pltpu.VMEM)

    def kernel(*refs):
        prep_kernel(tile_k, *refs)

    return pl.pallas_call(
        kernel,
        out_shape=(
            jax.ShapeDtypeStruct((2, k_width, rows // 2), jnp.int16),
            jax.ShapeDtypeStruct((1, tiles), I32),
            jax.ShapeDtypeStruct((owner_count, tile_rows, 128), BF16),
        ),
        in_specs=[pl.BlockSpec(memory_space=pltpu.SMEM)] + [vmem] * 5,
        out_specs=(vmem, vmem, vmem),
        compiler_params=pltpu.CompilerParams(vmem_limit_bytes=24 << 20),
        name="prep",
    )(where, amps_t, owners, amp_mask, keep_mask, energy)


def place_tiles(slot, h, first, acc, out_ref, to):
    tile_rows = out_ref.shape[3]
    for n in range(acc.shape[0] // tile_rows):
        at = slot[0, 2 * (first + n) + h]
        tile = acc[n * tile_rows : (n + 1) * tile_rows] * (1.0 / 128.0)
        out_ref[to, at // 2, at % 2] = tile.astype(BF16)


def near_kernel(slot, where, code_ref, ints_ref, amps_ref, out_ref):
    depth, rows = code_ref.shape
    block = depth // 8
    for k in range(0, depth, block):
        amps_ref[:, k : k + block] = decode(code_ref[k : k + block]).T
    tall = rows // 4
    for r in range(0, rows, tall):
        acc = dot(amps_ref[r : r + tall], ints_ref[...])
        place_tiles(slot, where[0], r // out_ref.shape[3], acc, out_ref, where[0])


def near(slot, where, code, ints, owner_count, tile_rows):
    depth, rows = code.shape
    width = ints.shape[1]
    smem = pl.BlockSpec(memory_space=pltpu.SMEM)
    vmem = pl.BlockSpec(memory_space=pltpu.VMEM)
    return pl.pallas_call(
        near_kernel,
        out_shape=(
            jax.ShapeDtypeStruct((rows, depth), BF16),
            jax.ShapeDtypeStruct((2, owner_count, 2, tile_rows, width), BF16),
        ),
        in_specs=[smem, smem, vmem, vmem],
        out_specs=(vmem, vmem),
        compiler_params=pltpu.CompilerParams(vmem_limit_bytes=NEAR_LIMIT << 20),
        cost_estimate=pl.CostEstimate(
            flops=2 * rows * depth * width, bytes_accessed=11 << 20, transcendentals=rows * depth
        ),
        name="near",
    )(slot, where, code, ints)


def far_kernel(slot, where, amps_ref, ints_hbm, _, out_ref, ints_ref, acc_ref, sems):
    rows, depth = amps_ref.shape
    parts = sems.shape[0]
    block = depth // parts
    reads = []
    for n in range(parts):
        at = pl.ds(n * block, block)
        reads.append(pltpu.make_async_copy(ints_hbm.at[at], ints_ref.at[at], sems.at[n]))
        reads[-1].start()
    tall = rows // 2
    for n in range(parts):
        reads[n].wait()
        at = pl.ds(n * block, block)
        for r in range(0, rows, tall):
            part = dot(amps_ref[r : r + tall, at], ints_ref[at])
            if n > 0:
                part += acc_ref[r : r + tall]
            if n < parts - 1:
                acc_ref[r : r + tall] = part
            else:
                place_tiles(slot, where[0], r // out_ref.shape[3], part, out_ref, 1 - where[0])


def far(slot, where, amps, ints, send):
    rows, depth = amps.shape
    width = ints.shape[1]
    smem = pl.BlockSpec(memory_space=pltpu.SMEM)
    vmem = pl.BlockSpec(memory_space=pltpu.VMEM)
    return pl.pallas_call(
        far_kernel,
        out_shape=jax.ShapeDtypeStruct(send.shape, BF16),
        in_specs=[smem, smem, vmem, pl.BlockSpec(memory_space=pl.ANY), vmem],
        out_specs=vmem,
        scratch_shapes=[
            pltpu.VMEM(ints.shape, BF16),
            pltpu.VMEM((rows, width), F32),
            pltpu.SemaphoreType.DMA((3,)),
        ],
        input_output_aliases={4: 0},
        compiler_params=pltpu.CompilerParams(vmem_limit_bytes=FAR_LIMIT << 20),
        cost_estimate=pl.CostEstimate(
            flops=2 * rows * depth * width, bytes_accessed=8 << 20, transcendentals=0
        ),
        name="far",
    )(slot, where, amps, ints, send)


def update_kernel(recv_ref, meta_ref, mix_ref, vir_ref, out_ref, weight_ref, new_ref, sems):
    tile_rows = mix_ref.shape[1]
    tall = weight_ref.shape[0]
    batch = tall // (4 * tile_rows)
    copies = jnp.where(iota((tall, tile_rows), 0) % tile_rows == iota((tall, tile_rows), 1), 1.0, 0.0).astype(BF16)
    wide = dot(dot(copies, mix_ref[0]).astype(BF16), copies, 1, 1)
    same = iota((tall, tall), 0) // tile_rows == iota((tall, tall), 1) // tile_rows
    weight_ref[...] = jnp.where(same, wide, 0.0).astype(BF16)
    writes = []
    for step in range(meta_ref.shape[0] // batch):
        tiles, energies = [], []
        for s in range(step * batch, (step + 1) * batch):
            meta = meta_ref[s].astype(F32)
            odd = meta[0:1, 4:5] > 0.5
            for k in range(4):
                energy = meta[:, k : k + 1]
                even_tile = recv_ref[k % 2, s, k // 2].astype(F32)
                odd_tile = recv_ref[(k + 1) % 2, s, k // 2].astype(F32)
                tile = jnp.where(odd, odd_tile, even_tile)
                tiles.append(jnp.where(energy != 0.0, tile, 0.0).astype(BF16))
                energies.append(energy)
        mixed = dot(weight_ref[...], jnp.concatenate(tiles, axis=0))
        new = mixed / (vir_ref[...] - jnp.concatenate(energies, axis=0))
        at = pl.ds(step * batch * 4, batch * 4)
        new_ref[at] = new.astype(BF16).reshape((batch * 4,) + new_ref.shape[1:])
        write = pltpu.make_async_copy(new_ref.at[at], out_ref.at[at], sems.at[step])
        write.start()
        writes.append(write)
    for write in writes:
        write.wait()


def update(recv, meta, mix, vir_energy):
    _, owner_count, two, tile_rows, width = recv.shape
    batch = 2
    vmem = pl.BlockSpec(memory_space=pltpu.VMEM)
    return pl.pallas_call(
        update_kernel,
        out_shape=jax.ShapeDtypeStruct((owner_count * 4, tile_rows, width), BF16),
        in_specs=[vmem] * 4,
        out_specs=pl.BlockSpec(memory_space=pl.ANY),
        scratch_shapes=[
            pltpu.VMEM((batch * 4 * tile_rows, batch * 4 * tile_rows), BF16),
            pltpu.VMEM((owner_count * 4, tile_rows, width), BF16),
            pltpu.SemaphoreType.DMA((owner_count // batch,)),
        ],
        compiler_params=pltpu.CompilerParams(vmem_limit_bytes=24 << 20),
        name="update",
    )(recv, meta, mix, vir_energy)


def shards(amps, ints, amp_mask, keep_mask, owners, occ_energy, vir_energy, mix):
    tiles_dev, k_tiles = amp_mask.shape
    rows, k_width = amps.shape
    tile_rows = rows // tiles_dev
    depth, width = ints.shape
    owner_count = lax.axis_size(OCC)
    h = lax.axis_index("yhi").astype(I32)
    c = lax.axis_index("core").astype(I32)
    kfirst = (lax.axis_index(VIR) * k_width).astype(I32)
    where = jnp.stack([h, c, kfirst])
    ints_far = lax.ppermute(ints, ("ylo", "yhi"), [(n, 3 - n) for n in range(4)])
    code, slot, meta = prep(
        where,
        amps.T,
        owners.T,
        amp_mask.T,
        keep_mask.T,
        occ_energy.reshape(8, rows // 8),
        depth // k_tiles,
        owner_count,
    )
    partner = lax.ppermute(code[1], "yhi", [(0, 1), (1, 0)])
    code = jnp.where(h == 0, jnp.concatenate([code[0], partner]), jnp.concatenate([partner, code[0]]))
    meta = lax.all_to_all(meta, OCC, 0, 0, tiled=True)
    code = lax.all_gather(code, "z", axis=0, tiled=True)
    decoded, send = near(slot, where, code, ints, owner_count, tile_rows)
    send = far(slot, where, decoded, ints_far, send)
    recv = lax.all_to_all(
        send.reshape(2 * owner_count, 2, tile_rows, width), ("yhi",) + OCC, 0, 0, tiled=True
    )
    recv = recv.reshape(2, owner_count, 2, tile_rows, width)
    return update(recv, meta, mix, vir_energy.reshape(1, width))


def solution(mesh):
    split = Mesh(mesh.devices.reshape(2, 4, 2, 16, 2), OCC + VIR)
    in_specs = (
        P(OCC, VIR),
        P(None, VIR),
        P(OCC, None),
        P(OCC, VIR),
        P(OCC, None),
        P(OCC),
        P(VIR),
        P(OCC, None, None),
    )
    return jax.shard_map(
        shards, mesh=split, in_specs=in_specs, out_specs=P(OCC, None, VIR), check_vma=False
    )
```

```python
import jax
import jax.numpy as jnp
from jax import lax
from jax.experimental import pallas as pl
from jax.experimental.pallas import tpu as pltpu
from jax.sharding import Mesh
from jax.sharding import PartitionSpec as P

OCC = ("ylo", "x", "core")
VIR = ("z", "yhi")
F32 = jnp.float32
BF16 = jnp.bfloat16
I32 = jnp.int32
PREP_LIMIT = 62
NEAR_LIMIT = 32
FAR_LIMIT = 32


def iota(shape, dim):
    return lax.broadcasted_iota(I32, shape, dim)


def dot(a, b, da=1, db=0):
    return lax.dot_general(a, b, (((da,), (db,)), ((), ())), preferred_element_type=F32)


def encode(v):
    a = jnp.abs(v)
    small = a < 2.0**-60
    b = jnp.where(small, a * 2.0**60, a)
    e = jnp.floor(jnp.log2(jnp.maximum(b, 2.0**-70)))
    q = b * jnp.exp2(7.0 - e)
    up = q >= 255.5
    down = q < 127.5
    q = q * jnp.where(up, 0.5, jnp.where(down, 2.0, 1.0))
    e = e + jnp.where(up, 1.0, jnp.where(down, -1.0, 0.0)) - jnp.where(small, 60.0, 0.0)
    code = (e + 127.0) * 128.0 + (jnp.floor(q + 0.5) - 128.0)
    code = jnp.where(a < 2.0**-126, 0.0, code)
    return jnp.where(v < 0.0, -code, code).astype(I32)


def decode(c):
    c = c.astype(I32)
    m = jnp.abs(c)
    v = ((m & 127) | 128).astype(F32) * jnp.exp2((m >> 7).astype(F32) - 127.0)
    v = jnp.where(m == 0, 0.0, v)
    return jnp.where(c < 0, -v, v).astype(BF16)


def prep_kernel(
    tile_k, where, amps_hbm, owners_hbm, mask_hbm, keep_hbm, energy_hbm, kept_ref, sent_ref, slot_ref, meta_ref,
    amps_ref, owners_ref, mask_ref, keep_ref, energy_ref, sems
):
    pairs = (
        (owners_hbm, owners_ref), (keep_hbm, keep_ref), (mask_hbm, mask_ref), (energy_hbm, energy_ref), (amps_hbm, amps_ref)
    )
    reads = [pltpu.make_async_copy(a, b, sems.at[n]) for n, (a, b) in enumerate(pairs)]
    for read in reads:
        read.start()
    for read in reads:
        read.wait()
    k_width, rows = amps_ref.shape
    k_tiles, tiles = mask_ref.shape
    owners = meta_ref.shape[0]
    tile_rows = rows // tiles
    half = rows // 2
    own_row = owners_ref[...].astype(F32)
    i = iota((tiles, tiles), 0)
    j = iota((tiles, tiles), 1)
    own = jnp.sum(jnp.where(i == j, own_row, 0.0), axis=1, keepdims=True)
    earlier = jnp.where((own_row == own) & (j < i), 1.0, 0.0)
    before = jnp.where(own_row < own, 1.0, 0.0)
    k = jnp.sum(earlier, axis=1, keepdims=True)
    rank = jnp.sum(before, axis=1, keepdims=True) + k
    place = own * 2.0 + jnp.where(k >= 2.0, 1.0, 0.0)
    slot_ref[...] = jnp.sum(
        jnp.where(rank == j.astype(F32), place, 0.0), axis=0, keepdims=True
    ).astype(I32)
    lane = iota((tiles, 128), 1)
    keep = jnp.sum(jnp.where(i == j, keep_ref[...].astype(F32), 0.0), axis=1, keepdims=True)
    cols = jnp.where(
        lane == 0, rank, jnp.where(lane == 1, own, jnp.where(lane == 2, k, keep))
    ).astype(BF16)
    spread = jnp.where(iota((rows, tiles), 0) // tile_rows == iota((rows, tiles), 1), 1.0, 0.0).astype(BF16)
    per_row = dot(spread, cols)
    per_col = dot(cols, spread, 0, 1)
    column_tile = (where[2] + iota((k_width, k_tiles), 0)) // tile_k
    select = jnp.where(column_tile == iota((k_width, k_tiles), 1), 1.0, 0.0).astype(BF16)
    present = dot(select, mask_ref[...].astype(F32).astype(BF16)).astype(BF16)
    present = dot(present, spread, 1, 1)
    masked = jnp.where(present > 0.5, amps_ref[...].astype(F32), 0.0).astype(BF16)
    r = per_row[:, 0:1].astype(I32)
    target = ((r + where[0]) % 2) * half + (r // 2) * tile_rows + iota((rows, 1), 0) % tile_rows
    moved = jnp.where(target == iota((rows, rows), 1), 1.0, 0.0).astype(BF16)
    code = encode(dot(masked, moved))
    kept_ref[...] = code[:, :half].astype(jnp.int16)
    sent_ref[...] = code[:, half:].astype(jnp.int16)
    energy = energy_ref[...].astype(F32)
    energy = jnp.concatenate([energy[n : n + 1] for n in range(energy.shape[0])], axis=1)
    energy = jnp.where(per_col[3:4] > 0.5, energy, 0.0)
    to = per_col[1:2].astype(I32) * tile_rows + iota((1, rows), 1) % tile_rows
    big = iota((owners * tile_rows, rows), 0)
    sent = jnp.where(big == to, energy, 0.0).astype(BF16)
    position = jnp.where(per_row[:, 2:3].astype(I32) == iota((rows, 128), 1), 1.0, 0.0).astype(BF16)
    meta = dot(sent, position)
    start = jnp.sum(
        jnp.where(own_row < (iota((owners * tile_rows, tiles), 0) // tile_rows).astype(F32), 1.0, 0.0),
        axis=1,
        keepdims=True,
    ).astype(I32)
    odd = (start % 2).astype(F32)
    meta = jnp.where(iota(meta.shape, 1) == 4, odd, meta)
    meta_ref[...] = meta.astype(BF16).reshape(meta_ref.shape)


def prep(where, amps_t, owners, amp_mask, keep_mask, energy, tile_k, owner_count):
    k_width, rows = amps_t.shape
    tiles = amp_mask.shape[1]
    tile_rows = rows // tiles
    vmem = pl.BlockSpec(memory_space=pltpu.VMEM)

    def kernel(*refs):
        prep_kernel(tile_k, *refs)

    return pl.pallas_call(
        kernel,
        out_shape=(
            jax.ShapeDtypeStruct((k_width, rows // 2), jnp.int16),
            jax.ShapeDtypeStruct((k_width, rows // 2), jnp.int16),
            jax.ShapeDtypeStruct((1, tiles), I32),
            jax.ShapeDtypeStruct((owner_count, tile_rows, 128), BF16),
        ),
        in_specs=[pl.BlockSpec(memory_space=pltpu.SMEM)] + [pl.BlockSpec(memory_space=pl.ANY)] * 5,
        out_specs=(vmem, vmem, vmem, vmem),
        scratch_shapes=[
            pltpu.VMEM(a.shape, a.dtype) for a in (amps_t, owners, amp_mask, keep_mask, energy)
        ] + [pltpu.SemaphoreType.DMA((5,))],
        compiler_params=pltpu.CompilerParams(vmem_limit_bytes=PREP_LIMIT << 20),
        name="prep",
    )(where, amps_t, owners, amp_mask, keep_mask, energy)


def place_tiles(slot, h, first, acc, out_ref, to):
    tile_rows = out_ref.shape[3]
    for n in range(acc.shape[0] // tile_rows):
        at = slot[0, 2 * (first + n) + h]
        tile = acc[n * tile_rows : (n + 1) * tile_rows] * (1.0 / 128.0)
        out_ref[to, at // 2, at % 2] = tile.astype(BF16)


def near_kernel(slot, where, code_ref, ints_ref, amps_ref, out_ref):
    depth, rows = code_ref.shape
    block = depth // 8
    for k in range(0, depth, block):
        amps_ref[:, k : k + block] = decode(code_ref[k : k + block]).T
    tall = rows // 4
    for r in range(0, rows, tall):
        acc = dot(amps_ref[r : r + tall], ints_ref[...])
        place_tiles(slot, where[0], r // out_ref.shape[3], acc, out_ref, where[0])


def near(slot, where, code, ints, owner_count, tile_rows):
    depth, rows = code.shape
    width = ints.shape[1]
    smem = pl.BlockSpec(memory_space=pltpu.SMEM)
    vmem = pl.BlockSpec(memory_space=pltpu.VMEM)
    return pl.pallas_call(
        near_kernel,
        out_shape=(
            jax.ShapeDtypeStruct((rows, depth), BF16),
            jax.ShapeDtypeStruct((2, owner_count, 2, tile_rows, width), BF16),
        ),
        in_specs=[smem, smem, vmem, vmem],
        out_specs=(vmem, vmem),
        compiler_params=pltpu.CompilerParams(vmem_limit_bytes=NEAR_LIMIT << 20),
        cost_estimate=pl.CostEstimate(
            flops=2 * rows * depth * width, bytes_accessed=11 << 20, transcendentals=rows * depth
        ),
        name="near",
    )(slot, where, code, ints)


def far_kernel(slot, where, amps_ref, ints_hbm, _, out_ref, ints_ref, acc_ref, sems):
    rows, depth = amps_ref.shape
    parts = sems.shape[0]
    block = depth // parts
    reads = []
    for n in range(parts):
        at = pl.ds(n * block, block)
        reads.append(pltpu.make_async_copy(ints_hbm.at[at], ints_ref.at[at], sems.at[n]))
        reads[-1].start()
    tall = rows // 2
    for n in range(parts):
        reads[n].wait()
        at = pl.ds(n * block, block)
        for r in range(0, rows, tall):
            part = dot(amps_ref[r : r + tall, at], ints_ref[at])
            if n > 0:
                part += acc_ref[r : r + tall]
            if n < parts - 1:
                acc_ref[r : r + tall] = part
            else:
                place_tiles(slot, where[0], r // out_ref.shape[3], part, out_ref, 1 - where[0])


def far(slot, where, amps, ints, send):
    rows, depth = amps.shape
    width = ints.shape[1]
    smem = pl.BlockSpec(memory_space=pltpu.SMEM)
    vmem = pl.BlockSpec(memory_space=pltpu.VMEM)
    return pl.pallas_call(
        far_kernel,
        out_shape=jax.ShapeDtypeStruct(send.shape, BF16),
        in_specs=[smem, smem, vmem, pl.BlockSpec(memory_space=pl.ANY), vmem],
        out_specs=vmem,
        scratch_shapes=[
            pltpu.VMEM(ints.shape, BF16),
            pltpu.VMEM((rows, width), F32),
            pltpu.SemaphoreType.DMA((3,)),
        ],
        input_output_aliases={4: 0},
        compiler_params=pltpu.CompilerParams(vmem_limit_bytes=FAR_LIMIT << 20),
        cost_estimate=pl.CostEstimate(
            flops=2 * rows * depth * width, bytes_accessed=8 << 20, transcendentals=0
        ),
        name="far",
    )(slot, where, amps, ints, send)


def update_kernel(recv_ref, meta_ref, mix_ref, vir_ref, out_ref, weight_ref, new_ref, sems):
    tile_rows = mix_ref.shape[1]
    tall = weight_ref.shape[0]
    batch = tall // (4 * tile_rows)
    copies = jnp.where(iota((tall, tile_rows), 0) % tile_rows == iota((tall, tile_rows), 1), 1.0, 0.0).astype(BF16)
    wide = dot(dot(copies, mix_ref[0]).astype(BF16), copies, 1, 1)
    same = iota((tall, tall), 0) // tile_rows == iota((tall, tall), 1) // tile_rows
    weight_ref[...] = jnp.where(same, wide, 0.0).astype(BF16)
    writes = []
    for step in range(meta_ref.shape[0] // batch):
        tiles, energies = [], []
        for s in range(step * batch, (step + 1) * batch):
            meta = meta_ref[s].astype(F32)
            odd = meta[0:1, 4:5] > 0.5
            for k in range(4):
                energy = meta[:, k : k + 1]
                even_tile = recv_ref[k % 2, s, k // 2].astype(F32)
                odd_tile = recv_ref[(k + 1) % 2, s, k // 2].astype(F32)
                tile = jnp.where(odd, odd_tile, even_tile)
                tiles.append(jnp.where(energy != 0.0, tile, 0.0).astype(BF16))
                energies.append(energy)
        mixed = dot(weight_ref[...], jnp.concatenate(tiles, axis=0))
        new = mixed / (vir_ref[...] - jnp.concatenate(energies, axis=0))
        at = pl.ds(step * batch * 4, batch * 4)
        new_ref[at] = new.astype(BF16).reshape((batch * 4,) + new_ref.shape[1:])
        write = pltpu.make_async_copy(new_ref.at[at], out_ref.at[at], sems.at[step])
        write.start()
        writes.append(write)
    for write in writes:
        write.wait()


def update(recv, meta, mix, vir_energy):
    _, owner_count, two, tile_rows, width = recv.shape
    batch = 2
    vmem = pl.BlockSpec(memory_space=pltpu.VMEM)
    return pl.pallas_call(
        update_kernel,
        out_shape=jax.ShapeDtypeStruct((owner_count * 4, tile_rows, width), BF16),
        in_specs=[vmem] * 4,
        out_specs=pl.BlockSpec(memory_space=pl.ANY),
        scratch_shapes=[
            pltpu.VMEM((batch * 4 * tile_rows, batch * 4 * tile_rows), BF16),
            pltpu.VMEM((owner_count * 4, tile_rows, width), BF16),
            pltpu.SemaphoreType.DMA((owner_count // batch,)),
        ],
        compiler_params=pltpu.CompilerParams(vmem_limit_bytes=24 << 20),
        name="update",
    )(recv, meta, mix, vir_energy)


def shards(amps, ints, amp_mask, keep_mask, owners, occ_energy, vir_energy, mix):
    tiles_dev, k_tiles = amp_mask.shape
    rows, k_width = amps.shape
    tile_rows = rows // tiles_dev
    depth, width = ints.shape
    owner_count = lax.axis_size(OCC)
    h = lax.axis_index("yhi").astype(I32)
    c = lax.axis_index("core").astype(I32)
    kfirst = (lax.axis_index(VIR) * k_width).astype(I32)
    where = jnp.stack([h, c, kfirst])
    ints_far = lax.ppermute(ints, ("ylo", "yhi"), [(n, 3 - n) for n in range(4)])
    code, partner, slot, meta = prep(
        where,
        amps.T,
        owners.T,
        amp_mask.T,
        keep_mask.T,
        occ_energy.reshape(8, rows // 8),
        depth // k_tiles,
        owner_count,
    )
    partner = lax.ppermute(partner, "yhi", [(0, 1), (1, 0)])
    code = jnp.where(h == 0, jnp.concatenate([code, partner]), jnp.concatenate([partner, code]))
    meta = lax.all_to_all(meta, OCC, 0, 0, tiled=True)
    code = lax.all_gather(code, "z", axis=0, tiled=True)
    decoded, send = near(slot, where, code, ints, owner_count, tile_rows)
    send = far(slot, where, decoded, ints_far, send)
    recv = lax.all_to_all(
        send.reshape(2 * owner_count, 2, tile_rows, width), ("yhi",) + OCC, 0, 0, tiled=True
    )
    recv = recv.reshape(2, owner_count, 2, tile_rows, width)
    return update(recv, meta, mix, vir_energy.reshape(1, width))


def solution(mesh):
    split = Mesh(mesh.devices.reshape(2, 4, 2, 16, 2), OCC + VIR)
    in_specs = (
        P(OCC, VIR),
        P(None, VIR),
        P(OCC, None),
        P(OCC, VIR),
        P(OCC, None),
        P(OCC),
        P(VIR),
        P(OCC, None, None),
    )
    return jax.shard_map(
        shards, mesh=split, in_specs=in_specs, out_specs=P(OCC, None, VIR), check_vma=False
    )
```

```python
import jax
import jax.numpy as jnp
from jax import lax
from jax.experimental import pallas as pl
from jax.experimental.pallas import tpu as pltpu
from jax.sharding import Mesh
from jax.sharding import PartitionSpec as P

OCC = ("ylo", "x", "core")
VIR = ("z", "yhi")
F32 = jnp.float32
BF16 = jnp.bfloat16
I32 = jnp.int32
PREP_LIMIT = 62
NEAR_LIMIT = 32
FAR_LIMIT = 32


def iota(shape, dim):
    return lax.broadcasted_iota(I32, shape, dim)


def dot(a, b, da=1, db=0):
    return lax.dot_general(a, b, (((da,), (db,)), ((), ())), preferred_element_type=F32)


def encode(v):
    a = jnp.abs(v)
    small = a < 2.0**-60
    b = jnp.where(small, a * 2.0**60, a)
    e = jnp.floor(jnp.log2(jnp.maximum(b, 2.0**-70)))
    q = b * jnp.exp2(7.0 - e)
    up = q >= 255.5
    down = q < 127.5
    q = q * jnp.where(up, 0.5, jnp.where(down, 2.0, 1.0))
    e = e + jnp.where(up, 1.0, jnp.where(down, -1.0, 0.0)) - jnp.where(small, 60.0, 0.0)
    code = (e + 127.0) * 128.0 + (jnp.floor(q + 0.5) - 128.0)
    code = jnp.where(a < 2.0**-126, 0.0, code)
    return jnp.where(v < 0.0, code - 32768.0, code).astype(I32)


def decode(c):
    c = c.astype(I32)
    m = (c & 127) | 128
    f = jnp.where(c < 0, -m, m)
    return (f.astype(F32) * jnp.exp2(((c >> 7) & 255).astype(F32) - 127.0)).astype(BF16)


def fetch(pairs, sems):
    reads = [pltpu.make_async_copy(a, b, sems.at[n]) for n, (a, b) in enumerate(pairs)]
    for read in reads:
        read.start()
    for read in reads:
        read.wait()


def rows_of_tiles(rows, tiles):
    return jnp.where(iota((rows, tiles), 0) // (rows // tiles) == iota((rows, tiles), 1), 1.0, 0.0).astype(BF16)


def as_column(row):
    n = row.shape[1]
    return jnp.sum(jnp.where(iota((n, n), 0) == iota((n, n), 1), row, 0.0), axis=1, keepdims=True)


def route_kernel(
    owners_hbm, keep_hbm, energy_hbm, rank_ref, slot_ref, meta_ref, owners_ref, keep_ref, energy_ref, sems
):
    fetch(((owners_hbm, owners_ref), (keep_hbm, keep_ref), (energy_hbm, energy_ref)), sems)
    tiles = owners_ref.shape[1]
    owners, tile_rows, _ = meta_ref.shape
    rows = tiles * tile_rows
    own_row = owners_ref[...].astype(F32)
    own = as_column(own_row)
    i = iota((tiles, tiles), 0)
    j = iota((tiles, tiles), 1)
    k = jnp.sum(jnp.where((own_row == own) & (j < i), 1.0, 0.0), axis=1, keepdims=True)
    rank = jnp.sum(jnp.where(own_row < own, 1.0, 0.0), axis=1, keepdims=True) + k
    rank_ref[...] = jnp.sum(jnp.where(i == j, rank, 0.0), axis=0, keepdims=True).astype(I32)
    place = own * 2.0 + jnp.where(k >= 2.0, 1.0, 0.0)
    slot_ref[...] = jnp.sum(
        jnp.where(rank == j.astype(F32), place, 0.0), axis=0, keepdims=True
    ).astype(I32)
    lane = iota((tiles, 128), 1)
    keep = as_column(keep_ref[...].astype(F32))
    cols = jnp.where(lane == 0, own, jnp.where(lane == 1, k, keep)).astype(BF16)
    spread = rows_of_tiles(rows, tiles)
    per_row = dot(spread, cols)
    per_col = dot(cols, spread, 0, 1)
    energy = energy_ref[...].astype(F32)
    energy = jnp.concatenate([energy[n : n + 1] for n in range(energy.shape[0])], axis=1)
    energy = jnp.where(per_col[2:3] > 0.5, energy, 0.0)
    to = per_col[0:1].astype(I32) * tile_rows + iota((1, rows), 1) % tile_rows
    big = iota((owners * tile_rows, rows), 0)
    sent = jnp.where(big == to, energy, 0.0).astype(BF16)
    position = jnp.where(per_row[:, 1:2].astype(I32) == iota((rows, 128), 1), 1.0, 0.0).astype(BF16)
    meta = dot(sent, position)
    start = jnp.sum(
        jnp.where(own_row < (iota((owners * tile_rows, tiles), 0) // tile_rows).astype(F32), 1.0, 0.0),
        axis=1,
        keepdims=True,
    ).astype(I32)
    odd = (start % 2).astype(F32)
    meta = jnp.where(iota(meta.shape, 1) == 4, odd, meta)
    meta_ref[...] = meta.astype(BF16).reshape(meta_ref.shape)


def route(owners, keep_mask, energy, owner_count):
    tiles = owners.shape[1]
    tile_rows = energy.size // tiles
    vmem = pl.BlockSpec(memory_space=pltpu.VMEM)
    return pl.pallas_call(
        route_kernel,
        out_shape=(
            jax.ShapeDtypeStruct((1, tiles), I32),
            jax.ShapeDtypeStruct((1, tiles), I32),
            jax.ShapeDtypeStruct((owner_count, tile_rows, 128), BF16),
        ),
        in_specs=[pl.BlockSpec(memory_space=pl.ANY)] * 3,
        out_specs=(vmem, vmem, vmem),
        scratch_shapes=[pltpu.VMEM(a.shape, a.dtype) for a in (owners, keep_mask, energy)]
        + [pltpu.SemaphoreType.DMA((3,))],
        compiler_params=pltpu.CompilerParams(vmem_limit_bytes=PREP_LIMIT << 20),
        name="route",
    )(owners, keep_mask, energy)


def order_kernel(tile_k, own_hbm, partner_hbm, rank_hbm, mask_hbm, code_ref, amps_ref, rank_ref, mask_ref, sems):
    h = lax.axis_index("yhi").astype(I32)
    z = lax.axis_index("z").astype(I32)
    k_width, rows = own_hbm.shape
    depth = 2 * k_width
    k_tiles, tiles = mask_ref.shape
    tile_rows = rows // tiles
    half = rows // 2
    mine = amps_ref.at[pl.ds(pl.multiple_of(h * k_width, 16), k_width)]
    other = amps_ref.at[pl.ds(pl.multiple_of((1 - h) * k_width, 16), k_width)]
    fetch(((rank_hbm, rank_ref), (mask_hbm, mask_ref), (own_hbm, mine), (partner_hbm, other)), sems)
    lane = iota((tiles, 128), 1)
    cols = jnp.where(lane == 0, as_column(rank_ref[...].astype(F32)), 0.0).astype(BF16)
    spread = rows_of_tiles(rows, tiles)
    r = dot(spread, cols)[:, 0:1].astype(I32)
    column_tile = (z * depth + iota((depth, k_tiles), 0)) // tile_k
    select = jnp.where(column_tile == iota((depth, k_tiles), 1), 1.0, 0.0).astype(BF16)
    present = dot(select, mask_ref[...].astype(F32).astype(BF16)).astype(BF16)
    present = dot(present, spread, 1, 1)
    masked = jnp.where(present > 0.5, amps_ref[...].astype(F32), 0.0).astype(BF16)
    target = ((r + h) % 2) * half + (r // 2) * tile_rows + iota((rows, 1), 0) % tile_rows
    moved = jnp.where(target == iota((rows, half), 1), 1.0, 0.0).astype(BF16)
    code_ref[...] = encode(dot(masked, moved)).astype(jnp.int16)


def order(own, partner, rank, amp_mask, tile_k):
    k_width, rows = own.shape
    any_space = pl.BlockSpec(memory_space=pl.ANY)

    def kernel(*refs):
        order_kernel(tile_k, *refs)

    return pl.pallas_call(
        kernel,
        out_shape=jax.ShapeDtypeStruct((2 * k_width, rows // 2), jnp.int16),
        in_specs=[any_space] * 4,
        out_specs=pl.BlockSpec(memory_space=pltpu.VMEM),
        scratch_shapes=[
            pltpu.VMEM((2 * k_width, rows), BF16),
            pltpu.VMEM(rank.shape, I32),
            pltpu.VMEM(amp_mask.shape, I32),
            pltpu.SemaphoreType.DMA((4,)),
        ],
        compiler_params=pltpu.CompilerParams(vmem_limit_bytes=PREP_LIMIT << 20),
        name="order",
    )(own, partner, rank, amp_mask)


def place_tiles(slot, h, first, acc, out_ref, to):
    tile_rows = out_ref.shape[3]
    for n in range(acc.shape[0] // tile_rows):
        at = slot[0, 2 * (first + n) + h]
        tile = acc[n * tile_rows : (n + 1) * tile_rows] * (1.0 / 128.0)
        out_ref[to, at // 2, at % 2] = tile.astype(BF16)


def near_kernel(slot, code_ref, ints_ref, amps_ref, out_ref):
    depth, rows = code_ref.shape
    block = depth // 8
    for k in range(0, depth, block):
        amps_ref[:, k : k + block] = decode(code_ref[k : k + block]).T
    h = lax.axis_index("yhi").astype(I32)
    tall = rows // 4
    for r in range(0, rows, tall):
        acc = dot(amps_ref[r : r + tall], ints_ref[...])
        place_tiles(slot, h, r // out_ref.shape[3], acc, out_ref, h)


def near(slot, code, ints, owner_count, tile_rows):
    depth, rows = code.shape
    width = ints.shape[1]
    smem = pl.BlockSpec(memory_space=pltpu.SMEM)
    vmem = pl.BlockSpec(memory_space=pltpu.VMEM)
    return pl.pallas_call(
        near_kernel,
        out_shape=(
            jax.ShapeDtypeStruct((rows, depth), BF16),
            jax.ShapeDtypeStruct((2, owner_count, 2, tile_rows, width), BF16),
        ),
        in_specs=[smem, vmem, vmem],
        out_specs=(vmem, vmem),
        compiler_params=pltpu.CompilerParams(vmem_limit_bytes=NEAR_LIMIT << 20),
        cost_estimate=pl.CostEstimate(
            flops=2 * rows * depth * width, bytes_accessed=11 << 20, transcendentals=rows * depth
        ),
        name="near",
    )(slot, code, ints)


def far_kernel(slot, amps_ref, ints_hbm, _, out_ref, ints_ref, acc_ref, sems):
    h = lax.axis_index("yhi").astype(I32)
    rows, depth = amps_ref.shape
    parts = sems.shape[0]
    block = depth // parts
    reads = []
    for n in range(parts):
        at = pl.ds(n * block, block)
        reads.append(pltpu.make_async_copy(ints_hbm.at[at], ints_ref.at[at], sems.at[n]))
        reads[-1].start()
    tall = rows // 2
    for n in range(parts):
        reads[n].wait()
        at = pl.ds(n * block, block)
        for r in range(0, rows, tall):
            part = dot(amps_ref[r : r + tall, at], ints_ref[at])
            if n > 0:
                part += acc_ref[r : r + tall]
            if n < parts - 1:
                acc_ref[r : r + tall] = part
            else:
                place_tiles(slot, h, r // out_ref.shape[3], part, out_ref, 1 - h)


def far(slot, amps, ints, send):
    rows, depth = amps.shape
    width = ints.shape[1]
    smem = pl.BlockSpec(memory_space=pltpu.SMEM)
    vmem = pl.BlockSpec(memory_space=pltpu.VMEM)
    return pl.pallas_call(
        far_kernel,
        out_shape=jax.ShapeDtypeStruct(send.shape, BF16),
        in_specs=[smem, vmem, pl.BlockSpec(memory_space=pl.ANY), vmem],
        out_specs=vmem,
        scratch_shapes=[
            pltpu.VMEM(ints.shape, BF16),
            pltpu.VMEM((rows, width), F32),
            pltpu.SemaphoreType.DMA((3,)),
        ],
        input_output_aliases={3: 0},
        compiler_params=pltpu.CompilerParams(vmem_limit_bytes=FAR_LIMIT << 20),
        cost_estimate=pl.CostEstimate(
            flops=2 * rows * depth * width, bytes_accessed=8 << 20, transcendentals=0
        ),
        name="far",
    )(slot, amps, ints, send)


def update_kernel(recv_ref, meta_ref, mix_ref, vir_ref, out_ref, weight_ref, new_ref, sems):
    tile_rows = mix_ref.shape[1]
    tall = weight_ref.shape[0]
    batch = tall // (4 * tile_rows)
    copies = jnp.where(iota((tall, tile_rows), 0) % tile_rows == iota((tall, tile_rows), 1), 1.0, 0.0).astype(BF16)
    wide = dot(dot(copies, mix_ref[0]).astype(BF16), copies, 1, 1)
    same = iota((tall, tall), 0) // tile_rows == iota((tall, tall), 1) // tile_rows
    weight_ref[...] = jnp.where(same, wide, 0.0).astype(BF16)
    writes = []
    for step in range(meta_ref.shape[0] // batch):
        tiles, energies = [], []
        for s in range(step * batch, (step + 1) * batch):
            meta = meta_ref[s].astype(F32)
            odd = meta[0:1, 4:5] > 0.5
            for k in range(4):
                energy = meta[:, k : k + 1]
                even_tile = recv_ref[k % 2, s, k // 2].astype(F32)
                odd_tile = recv_ref[(k + 1) % 2, s, k // 2].astype(F32)
                tile = jnp.where(odd, odd_tile, even_tile)
                tiles.append(jnp.where(energy != 0.0, tile, 0.0).astype(BF16))
                energies.append(energy)
        mixed = dot(weight_ref[...], jnp.concatenate(tiles, axis=0))
        new = mixed / (vir_ref[...] - jnp.concatenate(energies, axis=0))
        at = pl.ds(step * batch * 4, batch * 4)
        new_ref[at] = new.astype(BF16).reshape((batch * 4,) + new_ref.shape[1:])
        write = pltpu.make_async_copy(new_ref.at[at], out_ref.at[at], sems.at[step])
        write.start()
        writes.append(write)
    for write in writes:
        write.wait()


def update(recv, meta, mix, vir_energy):
    _, owner_count, two, tile_rows, width = recv.shape
    batch = 2
    vmem = pl.BlockSpec(memory_space=pltpu.VMEM)
    return pl.pallas_call(
        update_kernel,
        out_shape=jax.ShapeDtypeStruct((owner_count * 4, tile_rows, width), BF16),
        in_specs=[vmem] * 4,
        out_specs=pl.BlockSpec(memory_space=pl.ANY),
        scratch_shapes=[
            pltpu.VMEM((batch * 4 * tile_rows, batch * 4 * tile_rows), BF16),
            pltpu.VMEM((owner_count * 4, tile_rows, width), BF16),
            pltpu.SemaphoreType.DMA((owner_count // batch,)),
        ],
        compiler_params=pltpu.CompilerParams(vmem_limit_bytes=24 << 20),
        name="update",
    )(recv, meta, mix, vir_energy)


def shards(amps, ints, amp_mask, keep_mask, owners, occ_energy, vir_energy, mix):
    tiles_dev, k_tiles = amp_mask.shape
    rows, k_width = amps.shape
    tile_rows = rows // tiles_dev
    depth, width = ints.shape
    owner_count = lax.axis_size(OCC)
    ints_far = lax.ppermute(ints, ("ylo", "yhi"), [(n, 3 - n) for n in range(4)])
    partner = lax.ppermute(amps, "yhi", [(0, 1), (1, 0)])
    rank, slot, meta = route(owners.T, keep_mask.T, occ_energy.reshape(8, rows // 8), owner_count)
    meta = lax.all_to_all(meta, OCC, 0, 0, tiled=True)
    code = order(amps.T, partner.T, rank, amp_mask.T, depth // k_tiles)
    code = lax.all_gather(code, "z", axis=0, tiled=True)
    decoded, send = near(slot, code, ints, owner_count, tile_rows)
    send = far(slot, decoded, ints_far, send)
    recv = lax.all_to_all(
        send.reshape(2 * owner_count, 2, tile_rows, width), ("yhi",) + OCC, 0, 0, tiled=True
    )
    recv = recv.reshape(2, owner_count, 2, tile_rows, width)
    return update(recv, meta, mix, vir_energy.reshape(1, width))


def solution(mesh):
    split = Mesh(mesh.devices.reshape(2, 4, 2, 16, 2), OCC + VIR)
    in_specs = (
        P(OCC, VIR),
        P(None, VIR),
        P(OCC, None),
        P(OCC, VIR),
        P(OCC, None),
        P(OCC),
        P(VIR),
        P(OCC, None, None),
    )
    return jax.shard_map(
        shards, mesh=split, in_specs=in_specs, out_specs=P(OCC, None, VIR), check_vma=False
    )
```

```python
import jax
import jax.numpy as jnp
from jax import lax
from jax.experimental import pallas as pl
from jax.experimental.pallas import tpu as pltpu
from jax.sharding import Mesh
from jax.sharding import PartitionSpec as P

OCC = ("ylo", "x", "core")
VIR = ("z", "yhi")
F32 = jnp.float32
BF16 = jnp.bfloat16
I32 = jnp.int32
PREP_LIMIT = 62
NEAR_LIMIT = 32
FAR_LIMIT = 32


def iota(shape, dim):
    return lax.broadcasted_iota(I32, shape, dim)


def dot(a, b, da=1, db=0):
    return lax.dot_general(a, b, (((da,), (db,)), ((), ())), preferred_element_type=F32)


def encode(v):
    a = jnp.abs(v)
    small = a < 2.0**-60
    b = jnp.where(small, a * 2.0**60, a)
    e = jnp.floor(jnp.log2(jnp.maximum(b, 2.0**-70)))
    q = b * jnp.exp2(7.0 - e)
    up = q >= 255.5
    down = q < 127.5
    q = q * jnp.where(up, 0.5, jnp.where(down, 2.0, 1.0))
    e = e + jnp.where(up, 1.0, jnp.where(down, -1.0, 0.0)) - jnp.where(small, 60.0, 0.0)
    q = jnp.floor(q + 0.5)
    code = (e + 127.0) * 128.0 + jnp.where(v < 0.0, 255.0 - q - 32768.0, q - 128.0)
    return jnp.where(a < 2.0**-126, 0.0, code).astype(I32)


def decode(c):
    c = c.astype(I32)
    f = jnp.where(c < 0, -255, 128) + (c & 127)
    return (f.astype(F32) * jnp.exp2(((c >> 7) & 255).astype(F32) - 127.0)).astype(BF16)


def fetch(pairs, sems):
    reads = [pltpu.make_async_copy(a, b, sems.at[n]) for n, (a, b) in enumerate(pairs)]
    for read in reads:
        read.start()
    for read in reads:
        read.wait()


def rows_of_tiles(rows, tiles):
    return jnp.where(iota((rows, tiles), 0) // (rows // tiles) == iota((rows, tiles), 1), 1.0, 0.0).astype(BF16)


def as_column(row):
    n = row.shape[1]
    return jnp.sum(jnp.where(iota((n, n), 0) == iota((n, n), 1), row, 0.0), axis=1, keepdims=True)


def route_kernel(
    owners_hbm, keep_hbm, energy_hbm, ints_hbm, rank_ref, slot_ref, meta_ref, part_hbm,
    owners_ref, keep_ref, energy_ref, part_ref, sems
):
    part_rows = part_ref.shape[0]
    first = pl.multiple_of(lax.axis_index("core").astype(I32) * part_rows, part_rows)
    cut = pltpu.make_async_copy(ints_hbm.at[pl.ds(first, part_rows)], part_ref, sems.at[3])
    put = pltpu.make_async_copy(part_ref, part_hbm, sems.at[4])
    cut.start()
    fetch(((owners_hbm, owners_ref), (keep_hbm, keep_ref), (energy_hbm, energy_ref)), sems)
    tiles = owners_ref.shape[1]
    owners, tile_rows, _ = meta_ref.shape
    rows = tiles * tile_rows
    own_row = owners_ref[...].astype(F32)
    own = as_column(own_row)
    i = iota((tiles, tiles), 0)
    j = iota((tiles, tiles), 1)
    k = jnp.sum(jnp.where((own_row == own) & (j < i), 1.0, 0.0), axis=1, keepdims=True)
    rank = jnp.sum(jnp.where(own_row < own, 1.0, 0.0), axis=1, keepdims=True) + k
    rank_ref[...] = jnp.sum(jnp.where(i == j, rank, 0.0), axis=0, keepdims=True).astype(I32)
    place = own * 2.0 + jnp.where(k >= 2.0, 1.0, 0.0)
    slot_ref[...] = jnp.sum(
        jnp.where(rank == j.astype(F32), place, 0.0), axis=0, keepdims=True
    ).astype(I32)
    lane = iota((tiles, 128), 1)
    keep = as_column(keep_ref[...].astype(F32))
    cols = jnp.where(lane == 0, own, jnp.where(lane == 1, k, keep)).astype(BF16)
    spread = rows_of_tiles(rows, tiles)
    per_row = dot(spread, cols)
    per_col = dot(cols, spread, 0, 1)
    cut.wait()
    put.start()
    energy = energy_ref[...].astype(F32)
    energy = jnp.concatenate([energy[n : n + 1] for n in range(energy.shape[0])], axis=1)
    energy = jnp.where(per_col[2:3] > 0.5, energy, 0.0)
    to = per_col[0:1].astype(I32) * tile_rows + iota((1, rows), 1) % tile_rows
    big = iota((owners * tile_rows, rows), 0)
    sent = jnp.where(big == to, energy, 0.0).astype(BF16)
    position = jnp.where(per_row[:, 1:2].astype(I32) == iota((rows, 128), 1), 1.0, 0.0).astype(BF16)
    meta = dot(sent, position)
    start = jnp.sum(
        jnp.where(own_row < (iota((owners * tile_rows, tiles), 0) // tile_rows).astype(F32), 1.0, 0.0),
        axis=1,
        keepdims=True,
    ).astype(I32)
    odd = (start % 2).astype(F32)
    meta = jnp.where(iota(meta.shape, 1) == 4, odd, meta)
    meta_ref[...] = meta.astype(BF16).reshape(meta_ref.shape)
    put.wait()


def route(owners, keep_mask, energy, ints, owner_count):
    part = (ints.shape[0] // 2, ints.shape[1])
    any_space = pl.BlockSpec(memory_space=pl.ANY)
    tiles = owners.shape[1]
    tile_rows = energy.size // tiles
    vmem = pl.BlockSpec(memory_space=pltpu.VMEM)
    return pl.pallas_call(
        route_kernel,
        out_shape=(
            jax.ShapeDtypeStruct((1, tiles), I32),
            jax.ShapeDtypeStruct((1, tiles), I32),
            jax.ShapeDtypeStruct((owner_count, tile_rows, 128), BF16),
            jax.ShapeDtypeStruct(part, BF16),
        ),
        in_specs=[any_space] * 4,
        out_specs=(vmem, vmem, vmem, any_space),
        scratch_shapes=[pltpu.VMEM(a.shape, a.dtype) for a in (owners, keep_mask, energy)]
        + [pltpu.VMEM(part, BF16), pltpu.SemaphoreType.DMA((5,))],
        compiler_params=pltpu.CompilerParams(vmem_limit_bytes=PREP_LIMIT << 20),
        name="route",
    )(owners, keep_mask, energy, ints)


def order_kernel(tile_k, own_hbm, partner_hbm, rank_hbm, mask_hbm, code_ref, amps_ref, rank_ref, mask_ref, sems):
    h = lax.axis_index("yhi").astype(I32)
    z = lax.axis_index("z").astype(I32)
    k_width, rows = own_hbm.shape
    depth = 2 * k_width
    k_tiles, tiles = mask_ref.shape
    tile_rows = rows // tiles
    half = rows // 2
    mine = amps_ref.at[pl.ds(pl.multiple_of(h * k_width, 16), k_width)]
    other = amps_ref.at[pl.ds(pl.multiple_of((1 - h) * k_width, 16), k_width)]
    large = [
        pltpu.make_async_copy(own_hbm, mine, sems.at[2]), pltpu.make_async_copy(partner_hbm, other, sems.at[3])
    ]
    for read in large:
        read.start()
    fetch(((rank_hbm, rank_ref), (mask_hbm, mask_ref)), sems)
    lane = iota((tiles, 128), 1)
    cols = jnp.where(lane == 0, as_column(rank_ref[...].astype(F32)), 0.0).astype(BF16)
    spread = rows_of_tiles(rows, tiles)
    r = dot(spread, cols)[:, 0:1].astype(I32)
    column_tile = (z * depth + iota((depth, k_tiles), 0)) // tile_k
    select = jnp.where(column_tile == iota((depth, k_tiles), 1), 1.0, 0.0).astype(BF16)
    present = dot(select, mask_ref[...].astype(F32).astype(BF16)).astype(BF16)
    present = dot(present, spread, 1, 1)
    target = ((r + h) % 2) * half + (r // 2) * tile_rows + iota((rows, 1), 0) % tile_rows
    moved = jnp.where(target == iota((rows, half), 1), 1.0, 0.0).astype(BF16)
    for read in large:
        read.wait()
    masked = jnp.where(present > 0.5, amps_ref[...].astype(F32), 0.0).astype(BF16)
    code_ref[...] = encode(dot(masked, moved)).astype(jnp.int16)


def order(own, partner, rank, amp_mask, tile_k):
    k_width, rows = own.shape
    any_space = pl.BlockSpec(memory_space=pl.ANY)

    def kernel(*refs):
        order_kernel(tile_k, *refs)

    return pl.pallas_call(
        kernel,
        out_shape=jax.ShapeDtypeStruct((2 * k_width, rows // 2), jnp.int16),
        in_specs=[any_space] * 4,
        out_specs=pl.BlockSpec(memory_space=pltpu.VMEM),
        scratch_shapes=[
            pltpu.VMEM((2 * k_width, rows), BF16),
            pltpu.VMEM(rank.shape, I32),
            pltpu.VMEM(amp_mask.shape, I32),
            pltpu.SemaphoreType.DMA((4,)),
        ],
        compiler_params=pltpu.CompilerParams(vmem_limit_bytes=PREP_LIMIT << 20),
        name="order",
    )(own, partner, rank, amp_mask)


def place_tiles(slot, h, first, acc, out_ref, to):
    tile_rows = out_ref.shape[3]
    for n in range(acc.shape[0] // tile_rows):
        at = slot[0, 2 * (first + n) + h]
        tile = acc[n * tile_rows : (n + 1) * tile_rows] * (1.0 / 128.0)
        out_ref[to, at // 2, at % 2] = tile.astype(BF16)


def near_kernel(slot, code_ref, ints_ref, amps_ref, out_ref):
    depth, rows = code_ref.shape
    block = depth // 8
    for k in range(0, depth, block):
        amps_ref[:, k : k + block] = decode(code_ref[k : k + block]).T
    h = lax.axis_index("yhi").astype(I32)
    tall = rows // 4
    for r in range(0, rows, tall):
        acc = dot(amps_ref[r : r + tall], ints_ref[...])
        place_tiles(slot, h, r // out_ref.shape[3], acc, out_ref, h)


def near(slot, code, ints, owner_count, tile_rows):
    depth, rows = code.shape
    width = ints.shape[1]
    smem = pl.BlockSpec(memory_space=pltpu.SMEM)
    vmem = pl.BlockSpec(memory_space=pltpu.VMEM)
    return pl.pallas_call(
        near_kernel,
        out_shape=(
            jax.ShapeDtypeStruct((rows, depth), BF16),
            jax.ShapeDtypeStruct((2, owner_count, 2, tile_rows, width), BF16),
        ),
        in_specs=[smem, vmem, vmem],
        out_specs=(vmem, vmem),
        compiler_params=pltpu.CompilerParams(vmem_limit_bytes=NEAR_LIMIT << 20),
        cost_estimate=pl.CostEstimate(
            flops=2 * rows * depth * width, bytes_accessed=11 << 20, transcendentals=rows * depth
        ),
        name="near",
    )(slot, code, ints)


def far_kernel(slot, amps_ref, mine_hbm, other_ref, _, out_ref, mine_ref, acc_ref, sem):
    read = pltpu.make_async_copy(mine_hbm, mine_ref, sem)
    read.start()
    h = lax.axis_index("yhi").astype(I32)
    c = lax.axis_index("core").astype(I32)
    rows = amps_ref.shape[0]
    half = other_ref.shape[0]
    tall = rows // 2
    for r in range(0, rows, tall):
        at = pl.ds(pl.multiple_of((1 - c) * half, half), half)
        acc_ref[r : r + tall] = dot(amps_ref[r : r + tall, at], other_ref[...])
    read.wait()
    for r in range(0, rows, tall):
        at = pl.ds(pl.multiple_of(c * half, half), half)
        acc = acc_ref[r : r + tall] + dot(amps_ref[r : r + tall, at], mine_ref[...])
        place_tiles(slot, h, r // out_ref.shape[3], acc, out_ref, 1 - h)


def far(slot, amps, mine, other, send):
    rows, depth = amps.shape
    width = mine.shape[1]
    smem = pl.BlockSpec(memory_space=pltpu.SMEM)
    vmem = pl.BlockSpec(memory_space=pltpu.VMEM)
    return pl.pallas_call(
        far_kernel,
        out_shape=jax.ShapeDtypeStruct(send.shape, BF16),
        in_specs=[smem, vmem, pl.BlockSpec(memory_space=pl.ANY), vmem, vmem],
        out_specs=vmem,
        scratch_shapes=[
            pltpu.VMEM(mine.shape, BF16),
            pltpu.VMEM((rows, width), F32),
            pltpu.SemaphoreType.DMA,
        ],
        input_output_aliases={4: 0},
        compiler_params=pltpu.CompilerParams(vmem_limit_bytes=FAR_LIMIT << 20),
        cost_estimate=pl.CostEstimate(
            flops=2 * rows * depth * width, bytes_accessed=8 << 20, transcendentals=0
        ),
        name="far",
    )(slot, amps, mine, other, send)


def update_kernel(recv_ref, meta_ref, mix_ref, vir_ref, out_ref, weight_ref, new_ref, sems):
    tile_rows = mix_ref.shape[1]
    tall = weight_ref.shape[0]
    batch = tall // (4 * tile_rows)
    copies = jnp.where(iota((tall, tile_rows), 0) % tile_rows == iota((tall, tile_rows), 1), 1.0, 0.0).astype(BF16)
    wide = dot(dot(copies, mix_ref[0]).astype(BF16), copies, 1, 1)
    same = iota((tall, tall), 0) // tile_rows == iota((tall, tall), 1) // tile_rows
    weight_ref[...] = jnp.where(same, wide, 0.0).astype(BF16)
    writes = []
    for step in range(meta_ref.shape[0] // batch):
        tiles, energies = [], []
        for s in range(step * batch, (step + 1) * batch):
            meta = meta_ref[s].astype(F32)
            odd = meta[0:1, 4:5] > 0.5
            for k in range(4):
                energy = meta[:, k : k + 1]
                even_tile = recv_ref[k % 2, s, k // 2].astype(F32)
                odd_tile = recv_ref[(k + 1) % 2, s, k // 2].astype(F32)
                tile = jnp.where(odd, odd_tile, even_tile)
                tiles.append(jnp.where(energy != 0.0, tile, 0.0).astype(BF16))
                energies.append(energy)
        mixed = dot(weight_ref[...], jnp.concatenate(tiles, axis=0))
        new = mixed / (vir_ref[...] - jnp.concatenate(energies, axis=0))
        at = pl.ds(step * batch * 4, batch * 4)
        new_ref[at] = new.astype(BF16).reshape((batch * 4,) + new_ref.shape[1:])
        write = pltpu.make_async_copy(new_ref.at[at], out_ref.at[at], sems.at[step])
        write.start()
        writes.append(write)
    for write in writes:
        write.wait()


def update(recv, meta, mix, vir_energy):
    _, owner_count, two, tile_rows, width = recv.shape
    batch = 2
    vmem = pl.BlockSpec(memory_space=pltpu.VMEM)
    return pl.pallas_call(
        update_kernel,
        out_shape=jax.ShapeDtypeStruct((owner_count * 4, tile_rows, width), BF16),
        in_specs=[vmem] * 4,
        out_specs=pl.BlockSpec(memory_space=pl.ANY),
        scratch_shapes=[
            pltpu.VMEM((batch * 4 * tile_rows, batch * 4 * tile_rows), BF16),
            pltpu.VMEM((owner_count * 4, tile_rows, width), BF16),
            pltpu.SemaphoreType.DMA((owner_count // batch,)),
        ],
        compiler_params=pltpu.CompilerParams(vmem_limit_bytes=24 << 20),
        name="update",
    )(recv, meta, mix, vir_energy)


def shards(amps, ints, amp_mask, keep_mask, owners, occ_energy, vir_energy, mix):
    tiles_dev, k_tiles = amp_mask.shape
    rows, k_width = amps.shape
    tile_rows = rows // tiles_dev
    depth, width = ints.shape
    owner_count = lax.axis_size(OCC)
    partner = lax.ppermute(amps, "yhi", [(0, 1), (1, 0)])
    rank, slot, meta, part = route(
        owners.T, keep_mask.T, occ_energy.reshape(8, rows // 8), ints, owner_count
    )
    meta = lax.all_to_all(meta, OCC, 0, 0, tiled=True)
    mine = lax.ppermute(part, ("ylo", "yhi"), [(n, 3 - n) for n in range(4)])
    code = order(amps.T, partner.T, rank, amp_mask.T, depth // k_tiles)
    code, meta = lax.optimization_barrier((code, meta))
    code = lax.all_gather(code, "z", axis=0, tiled=True)
    mine, code = lax.optimization_barrier((mine, code))
    other = lax.ppermute(mine, "core", [(0, 1), (1, 0)])
    decoded, send = near(slot, code, ints, owner_count, tile_rows)
    send = far(slot, decoded, mine, other, send)
    recv = lax.all_to_all(
        send.reshape(2 * owner_count, 2, tile_rows, width), ("yhi",) + OCC, 0, 0, tiled=True
    )
    recv = recv.reshape(2, owner_count, 2, tile_rows, width)
    return update(recv, meta, mix, vir_energy.reshape(1, width))


def solution(mesh):
    split = Mesh(mesh.devices.reshape(2, 4, 2, 16, 2), OCC + VIR)
    in_specs = (
        P(OCC, VIR),
        P(None, VIR),
        P(OCC, None),
        P(OCC, VIR),
        P(OCC, None),
        P(OCC),
        P(VIR),
        P(OCC, None, None),
    )
    return jax.shard_map(
        shards, mesh=split, in_specs=in_specs, out_specs=P(OCC, None, VIR), check_vma=False
    )
```

```python
import jax
import jax.numpy as jnp
from jax import lax
from jax.experimental import pallas as pl
from jax.experimental.pallas import tpu as pltpu
from jax.sharding import Mesh
from jax.sharding import PartitionSpec as P

OCC = ("ylo", "x", "core")
VIR = ("z", "yhi")
F32 = jnp.float32
BF16 = jnp.bfloat16
I32 = jnp.int32
PREP_LIMIT = 62
NEAR_LIMIT = 32


def iota(shape, dim):
    return lax.broadcasted_iota(I32, shape, dim)


def dot(a, b, da=1, db=0):
    return lax.dot_general(a, b, (((da,), (db,)), ((), ())), preferred_element_type=F32)


def encode(v):
    a = jnp.abs(v)
    small = a < 2.0**-60
    b = jnp.where(small, a * 2.0**60, a)
    e = jnp.floor(jnp.log2(jnp.maximum(b, 2.0**-70)))
    q = b * jnp.exp2(7.0 - e)
    up = q >= 255.5
    down = q < 127.5
    q = q * jnp.where(up, 0.5, jnp.where(down, 2.0, 1.0))
    e = e + jnp.where(up, 1.0, jnp.where(down, -1.0, 0.0)) - jnp.where(small, 60.0, 0.0)
    q = jnp.floor(q + 0.5)
    code = (e + 127.0) * 128.0 + jnp.where(v < 0.0, 255.0 - q - 32768.0, q - 128.0)
    return jnp.where(a < 2.0**-126, 0.0, code).astype(I32)


def decode(c):
    c = c.astype(I32)
    f = jnp.where(c < 0, -255, 128) + (c & 127)
    return (f.astype(F32) * jnp.exp2(((c >> 7) & 255).astype(F32) - 127.0)).astype(BF16)


def fetch(pairs, sems):
    reads = [pltpu.make_async_copy(a, b, sems.at[n]) for n, (a, b) in enumerate(pairs)]
    for read in reads:
        read.start()
    for read in reads:
        read.wait()


def rows_of_tiles(rows, tiles):
    return jnp.where(iota((rows, tiles), 0) // (rows // tiles) == iota((rows, tiles), 1), 1.0, 0.0).astype(BF16)


def as_column(row):
    n = row.shape[1]
    return jnp.sum(jnp.where(iota((n, n), 0) == iota((n, n), 1), row, 0.0), axis=1, keepdims=True)


def route_kernel(
    owners_hbm, keep_hbm, energy_hbm, rank_ref, slot_ref, meta_ref, owners_ref, keep_ref, energy_ref, sems
):
    fetch(((owners_hbm, owners_ref), (keep_hbm, keep_ref), (energy_hbm, energy_ref)), sems)
    tiles = owners_ref.shape[1]
    owners, tile_rows, _ = meta_ref.shape
    rows = tiles * tile_rows
    own_row = owners_ref[...].astype(F32)
    own = as_column(own_row)
    i = iota((tiles, tiles), 0)
    j = iota((tiles, tiles), 1)
    k = jnp.sum(jnp.where((own_row == own) & (j < i), 1.0, 0.0), axis=1, keepdims=True)
    rank = jnp.sum(jnp.where(own_row < own, 1.0, 0.0), axis=1, keepdims=True) + k
    rank_ref[...] = jnp.sum(jnp.where(i == j, rank, 0.0), axis=0, keepdims=True).astype(I32)
    place = own * 2.0 + jnp.where(k >= 2.0, 1.0, 0.0)
    slot_ref[...] = jnp.sum(
        jnp.where(rank == j.astype(F32), place, 0.0), axis=0, keepdims=True
    ).astype(I32)
    lane = iota((tiles, 128), 1)
    keep = as_column(keep_ref[...].astype(F32))
    cols = jnp.where(lane == 0, own, jnp.where(lane == 1, k, keep)).astype(BF16)
    spread = rows_of_tiles(rows, tiles)
    per_row = dot(spread, cols)
    per_col = dot(cols, spread, 0, 1)
    energy = energy_ref[...].astype(F32)
    energy = jnp.concatenate([energy[n : n + 1] for n in range(energy.shape[0])], axis=1)
    energy = jnp.where(per_col[2:3] > 0.5, energy, 0.0)
    to = per_col[0:1].astype(I32) * tile_rows + iota((1, rows), 1) % tile_rows
    big = iota((owners * tile_rows, rows), 0)
    sent = jnp.where(big == to, energy, 0.0).astype(BF16)
    position = jnp.where(per_row[:, 1:2].astype(I32) == iota((rows, 128), 1), 1.0, 0.0).astype(BF16)
    meta = dot(sent, position)
    start = jnp.sum(
        jnp.where(own_row < (iota((owners * tile_rows, tiles), 0) // tile_rows).astype(F32), 1.0, 0.0),
        axis=1,
        keepdims=True,
    ).astype(I32)
    odd = (start % 2).astype(F32)
    meta = jnp.where(iota(meta.shape, 1) == 4, odd, meta)
    meta_ref[...] = meta.astype(BF16).reshape(meta_ref.shape)


def route(owners, keep_mask, energy, owner_count):
    tiles = owners.shape[1]
    tile_rows = energy.size // tiles
    vmem = pl.BlockSpec(memory_space=pltpu.VMEM)
    return pl.pallas_call(
        route_kernel,
        out_shape=(
            jax.ShapeDtypeStruct((1, tiles), I32),
            jax.ShapeDtypeStruct((1, tiles), I32),
            jax.ShapeDtypeStruct((owner_count, tile_rows, 128), BF16),
        ),
        in_specs=[pl.BlockSpec(memory_space=pl.ANY)] * 3,
        out_specs=(vmem, vmem, vmem),
        scratch_shapes=[pltpu.VMEM(a.shape, a.dtype) for a in (owners, keep_mask, energy)]
        + [pltpu.SemaphoreType.DMA((3,))],
        compiler_params=pltpu.CompilerParams(vmem_limit_bytes=PREP_LIMIT << 20),
        name="route",
    )(owners, keep_mask, energy)


def order_kernel(tile_k, own_hbm, partner_hbm, rank_hbm, mask_hbm, code_ref, amps_ref, rank_ref, mask_ref, sems):
    h = lax.axis_index("yhi").astype(I32)
    z = lax.axis_index("z").astype(I32)
    k_width, rows = own_hbm.shape
    depth = 2 * k_width
    k_tiles, tiles = mask_ref.shape
    tile_rows = rows // tiles
    half = rows // 2
    mine = amps_ref.at[pl.ds(pl.multiple_of(h * k_width, 16), k_width)]
    other = amps_ref.at[pl.ds(pl.multiple_of((1 - h) * k_width, 16), k_width)]
    large = [
        pltpu.make_async_copy(own_hbm, mine, sems.at[2]), pltpu.make_async_copy(partner_hbm, other, sems.at[3])
    ]
    for read in large:
        read.start()
    fetch(((rank_hbm, rank_ref), (mask_hbm, mask_ref)), sems)
    lane = iota((tiles, 128), 1)
    cols = jnp.where(lane == 0, as_column(rank_ref[...].astype(F32)), 0.0).astype(BF16)
    spread = rows_of_tiles(rows, tiles)
    r = dot(spread, cols)[:, 0:1].astype(I32)
    column_tile = (z * depth + iota((depth, k_tiles), 0)) // tile_k
    select = jnp.where(column_tile == iota((depth, k_tiles), 1), 1.0, 0.0).astype(BF16)
    present = dot(select, mask_ref[...].astype(F32).astype(BF16)).astype(BF16)
    present = dot(present, spread, 1, 1)
    target = ((r + h) % 2) * half + (r // 2) * tile_rows + iota((rows, 1), 0) % tile_rows
    moved = jnp.where(target == iota((rows, half), 1), 1.0, 0.0).astype(BF16)
    for read in large:
        read.wait()
    masked = jnp.where(present > 0.5, amps_ref[...].astype(F32), 0.0).astype(BF16)
    code_ref[...] = encode(dot(masked, moved)).astype(jnp.int16)


def order(own, partner, rank, amp_mask, tile_k):
    k_width, rows = own.shape
    any_space = pl.BlockSpec(memory_space=pl.ANY)

    def kernel(*refs):
        order_kernel(tile_k, *refs)

    return pl.pallas_call(
        kernel,
        out_shape=jax.ShapeDtypeStruct((2 * k_width, rows // 2), jnp.int16),
        in_specs=[any_space] * 4,
        out_specs=pl.BlockSpec(memory_space=pltpu.VMEM),
        scratch_shapes=[
            pltpu.VMEM((2 * k_width, rows), BF16),
            pltpu.VMEM(rank.shape, I32),
            pltpu.VMEM(amp_mask.shape, I32),
            pltpu.SemaphoreType.DMA((4,)),
        ],
        compiler_params=pltpu.CompilerParams(vmem_limit_bytes=PREP_LIMIT << 20),
        name="order",
    )(own, partner, rank, amp_mask)


def place_tiles(slot, h, first, acc, out_ref, to):
    tile_rows = out_ref.shape[3]
    for n in range(acc.shape[0] // tile_rows):
        at = slot[0, 2 * (first + n) + h]
        tile = acc[n * tile_rows : (n + 1) * tile_rows] * (1.0 / 128.0)
        out_ref[to, at // 2, at % 2] = tile.astype(BF16)


def ladder_kernel(slot, code_ref, ints_ref, far_hbm, out_ref, amps_ref, far_ref, sem):
    read = pltpu.make_async_copy(far_hbm, far_ref, sem)
    read.start()
    h = lax.axis_index("yhi").astype(I32)
    depth, rows = code_ref.shape
    tile_rows = out_ref.shape[3]
    block = depth // 4
    for k in range(0, depth, block):
        amps_ref[:, k : k + block] = decode(code_ref[k : k + block]).T
    tall = rows // 2
    for r in range(0, rows, tall):
        acc = dot(amps_ref[r : r + tall], ints_ref[...])
        place_tiles(slot, h, r // tile_rows, acc, out_ref, h)
    read.wait()
    for r in range(0, rows, tall):
        acc = dot(amps_ref[r : r + tall], far_ref[...])
        place_tiles(slot, h, r // tile_rows, acc, out_ref, 1 - h)


def ladder(slot, code, ints, ints_far, owner_count, tile_rows):
    depth, rows = code.shape
    width = ints.shape[1]
    smem = pl.BlockSpec(memory_space=pltpu.SMEM)
    vmem = pl.BlockSpec(memory_space=pltpu.VMEM)
    return pl.pallas_call(
        ladder_kernel,
        out_shape=jax.ShapeDtypeStruct((2, owner_count, 2, tile_rows, width), BF16),
        in_specs=[smem, vmem, vmem, pl.BlockSpec(memory_space=pl.ANY)],
        out_specs=vmem,
        scratch_shapes=[
            pltpu.VMEM((rows, depth), BF16),
            pltpu.VMEM(ints.shape, BF16),
            pltpu.SemaphoreType.DMA,
        ],
        compiler_params=pltpu.CompilerParams(vmem_limit_bytes=NEAR_LIMIT << 20),
        cost_estimate=pl.CostEstimate(
            flops=4 * rows * depth * width, bytes_accessed=11 << 20, transcendentals=rows * depth
        ),
        name="ladder",
    )(slot, code, ints, ints_far)


def update_kernel(recv_ref, meta_ref, mix_ref, vir_ref, out_ref, weight_ref, new_ref, sems):
    tile_rows = mix_ref.shape[1]
    tall = weight_ref.shape[0]
    batch = tall // (4 * tile_rows)
    copies = jnp.where(iota((tall, tile_rows), 0) % tile_rows == iota((tall, tile_rows), 1), 1.0, 0.0).astype(BF16)
    wide = dot(dot(copies, mix_ref[0]).astype(BF16), copies, 1, 1)
    same = iota((tall, tall), 0) // tile_rows == iota((tall, tall), 1) // tile_rows
    weight_ref[...] = jnp.where(same, wide, 0.0).astype(BF16)
    writes = []
    for step in range(meta_ref.shape[0] // batch):
        tiles, energies = [], []
        for s in range(step * batch, (step + 1) * batch):
            meta = meta_ref[s].astype(F32)
            odd = meta[0:1, 4:5] > 0.5
            for k in range(4):
                energy = meta[:, k : k + 1]
                even_tile = recv_ref[k % 2, s, k // 2].astype(F32)
                odd_tile = recv_ref[(k + 1) % 2, s, k // 2].astype(F32)
                tile = jnp.where(odd, odd_tile, even_tile)
                tiles.append(jnp.where(energy != 0.0, tile, 0.0).astype(BF16))
                energies.append(energy)
        mixed = dot(weight_ref[...], jnp.concatenate(tiles, axis=0))
        new = mixed / (vir_ref[...] - jnp.concatenate(energies, axis=0))
        at = pl.ds(step * batch * 4, batch * 4)
        new_ref[at] = new.astype(BF16).reshape((batch * 4,) + new_ref.shape[1:])
        write = pltpu.make_async_copy(new_ref.at[at], out_ref.at[at], sems.at[step])
        write.start()
        writes.append(write)
    for write in writes:
        write.wait()


def update(recv, meta, mix, vir_energy):
    _, owner_count, two, tile_rows, width = recv.shape
    batch = 2
    vmem = pl.BlockSpec(memory_space=pltpu.VMEM)
    return pl.pallas_call(
        update_kernel,
        out_shape=jax.ShapeDtypeStruct((owner_count * 4, tile_rows, width), BF16),
        in_specs=[vmem] * 4,
        out_specs=pl.BlockSpec(memory_space=pl.ANY),
        scratch_shapes=[
            pltpu.VMEM((batch * 4 * tile_rows, batch * 4 * tile_rows), BF16),
            pltpu.VMEM((owner_count * 4, tile_rows, width), BF16),
            pltpu.SemaphoreType.DMA((owner_count // batch,)),
        ],
        compiler_params=pltpu.CompilerParams(vmem_limit_bytes=24 << 20),
        name="update",
    )(recv, meta, mix, vir_energy)


def shards(amps, ints, amp_mask, keep_mask, owners, occ_energy, vir_energy, mix):
    tiles_dev, k_tiles = amp_mask.shape
    rows, k_width = amps.shape
    tile_rows = rows // tiles_dev
    depth, width = ints.shape
    owner_count = lax.axis_size(OCC)
    ints_far = lax.ppermute(ints, ("ylo", "yhi"), [(n, 3 - n) for n in range(4)])
    partner = lax.ppermute(amps, "yhi", [(0, 1), (1, 0)])
    rank, slot, meta = route(owners.T, keep_mask.T, occ_energy.reshape(8, rows // 8), owner_count)
    meta = lax.all_to_all(meta, OCC, 0, 0, tiled=True)
    code = order(amps.T, partner.T, rank, amp_mask.T, depth // k_tiles)
    code = lax.all_gather(code, "z", axis=0, tiled=True)
    send = ladder(slot, code, ints, ints_far, owner_count, tile_rows)
    recv = lax.all_to_all(
        send.reshape(2 * owner_count, 2, tile_rows, width), ("yhi",) + OCC, 0, 0, tiled=True
    )
    recv = recv.reshape(2, owner_count, 2, tile_rows, width)
    return update(recv, meta, mix, vir_energy.reshape(1, width))


def solution(mesh):
    split = Mesh(mesh.devices.reshape(2, 4, 2, 16, 2), OCC + VIR)
    in_specs = (
        P(OCC, VIR),
        P(None, VIR),
        P(OCC, None),
        P(OCC, VIR),
        P(OCC, None),
        P(OCC),
        P(VIR),
        P(OCC, None, None),
    )
    return jax.shard_map(
        shards, mesh=split, in_specs=in_specs, out_specs=P(OCC, None, VIR), check_vma=False
    )
```

```python
import jax
import jax.numpy as jnp
from jax import lax
from jax.experimental import pallas as pl
from jax.experimental.pallas import tpu as pltpu
from jax.sharding import Mesh
from jax.sharding import PartitionSpec as P

OCC = ("ylo", "x", "core")
VIR = ("z", "yhi")
F32 = jnp.float32
BF16 = jnp.bfloat16
I32 = jnp.int32
PREP_LIMIT = 62
NEAR_LIMIT = 32
FAR_LIMIT = 32


def iota(shape, dim):
    return lax.broadcasted_iota(I32, shape, dim)


def dot(a, b, da=1, db=0):
    return lax.dot_general(a, b, (((da,), (db,)), ((), ())), preferred_element_type=F32)


def encode(v):
    a = jnp.abs(v)
    small = a < 2.0**-60
    b = jnp.where(small, a * 2.0**60, a)
    e = jnp.floor(jnp.log2(jnp.maximum(b, 2.0**-70)))
    q = b * jnp.exp2(7.0 - e)
    up = q >= 255.5
    down = q < 127.5
    q = q * jnp.where(up, 0.5, jnp.where(down, 2.0, 1.0))
    e = e + jnp.where(up, 1.0, jnp.where(down, -1.0, 0.0)) - jnp.where(small, 60.0, 0.0)
    q = jnp.floor(q + 0.5)
    code = (e + 127.0) * 128.0 + jnp.where(v < 0.0, 255.0 - q - 32768.0, q - 128.0)
    return jnp.where(a < 2.0**-126, 0.0, code).astype(I32)


def decode(c):
    c = c.astype(I32)
    f = jnp.where(c < 0, -255, 128) + (c & 127)
    return (f.astype(F32) * jnp.exp2(((c >> 7) & 255).astype(F32) - 127.0)).astype(BF16)


def fetch(pairs, sems):
    reads = [pltpu.make_async_copy(a, b, sems.at[n]) for n, (a, b) in enumerate(pairs)]
    for read in reads:
        read.start()
    for read in reads:
        read.wait()


def rows_of_tiles(rows, tiles):
    return jnp.where(iota((rows, tiles), 0) // (rows // tiles) == iota((rows, tiles), 1), 1.0, 0.0).astype(BF16)


def as_column(row):
    n = row.shape[1]
    return jnp.sum(jnp.where(iota((n, n), 0) == iota((n, n), 1), row, 0.0), axis=1, keepdims=True)


def route_kernel(
    owners_hbm, keep_hbm, energy_hbm, rank_ref, slot_ref, meta_ref, owners_ref, keep_ref, energy_ref, sems
):
    fetch(((owners_hbm, owners_ref), (keep_hbm, keep_ref), (energy_hbm, energy_ref)), sems)
    tiles = owners_ref.shape[1]
    owners, tile_rows, _ = meta_ref.shape
    rows = tiles * tile_rows
    own_row = owners_ref[...].astype(F32)
    own = as_column(own_row)
    i = iota((tiles, tiles), 0)
    j = iota((tiles, tiles), 1)
    k = jnp.sum(jnp.where((own_row == own) & (j < i), 1.0, 0.0), axis=1, keepdims=True)
    rank = jnp.sum(jnp.where(own_row < own, 1.0, 0.0), axis=1, keepdims=True) + k
    rank_ref[...] = jnp.sum(jnp.where(i == j, rank, 0.0), axis=0, keepdims=True).astype(I32)
    place = own * 2.0 + jnp.where(k >= 2.0, 1.0, 0.0)
    slot_ref[...] = jnp.sum(
        jnp.where(rank == j.astype(F32), place, 0.0), axis=0, keepdims=True
    ).astype(I32)
    lane = iota((tiles, 128), 1)
    keep = as_column(keep_ref[...].astype(F32))
    cols = jnp.where(lane == 0, own, jnp.where(lane == 1, k, keep)).astype(BF16)
    spread = rows_of_tiles(rows, tiles)
    per_row = dot(spread, cols)
    per_col = dot(cols, spread, 0, 1)
    energy = energy_ref[...].astype(F32)
    energy = jnp.concatenate([energy[n : n + 1] for n in range(energy.shape[0])], axis=1)
    energy = jnp.where(per_col[2:3] > 0.5, energy, 0.0)
    to = per_col[0:1].astype(I32) * tile_rows + iota((1, rows), 1) % tile_rows
    big = iota((owners * tile_rows, rows), 0)
    sent = jnp.where(big == to, energy, 0.0).astype(BF16)
    position = jnp.where(per_row[:, 1:2].astype(I32) == iota((rows, 128), 1), 1.0, 0.0).astype(BF16)
    meta = dot(sent, position)
    start = jnp.sum(
        jnp.where(own_row < (iota((owners * tile_rows, tiles), 0) // tile_rows).astype(F32), 1.0, 0.0),
        axis=1,
        keepdims=True,
    ).astype(I32)
    odd = (start % 2).astype(F32)
    meta = jnp.where(iota(meta.shape, 1) == 4, odd, meta)
    meta_ref[...] = meta.astype(BF16).reshape(meta_ref.shape)


def route(owners, keep_mask, energy, owner_count):
    tiles = owners.shape[1]
    tile_rows = energy.size // tiles
    vmem = pl.BlockSpec(memory_space=pltpu.VMEM)
    return pl.pallas_call(
        route_kernel,
        out_shape=(
            jax.ShapeDtypeStruct((1, tiles), I32),
            jax.ShapeDtypeStruct((1, tiles), I32),
            jax.ShapeDtypeStruct((owner_count, tile_rows, 128), BF16),
        ),
        in_specs=[pl.BlockSpec(memory_space=pl.ANY)] * 3,
        out_specs=(vmem, vmem, vmem),
        scratch_shapes=[pltpu.VMEM(a.shape, a.dtype) for a in (owners, keep_mask, energy)]
        + [pltpu.SemaphoreType.DMA((3,))],
        compiler_params=pltpu.CompilerParams(vmem_limit_bytes=PREP_LIMIT << 20),
        name="route",
    )(owners, keep_mask, energy)


def order_kernel(tile_k, own_hbm, partner_hbm, rank_hbm, mask_hbm, code_ref, amps_ref, rank_ref, mask_ref, sems):
    h = lax.axis_index("yhi").astype(I32)
    z = lax.axis_index("z").astype(I32)
    k_width, rows = own_hbm.shape
    depth = 2 * k_width
    k_tiles, tiles = mask_ref.shape
    tile_rows = rows // tiles
    half = rows // 2
    mine = amps_ref.at[pl.ds(pl.multiple_of(h * k_width, 16), k_width)]
    other = amps_ref.at[pl.ds(pl.multiple_of((1 - h) * k_width, 16), k_width)]
    large = [
        pltpu.make_async_copy(own_hbm, mine, sems.at[2]), pltpu.make_async_copy(partner_hbm, other, sems.at[3])
    ]
    for read in large:
        read.start()
    fetch(((rank_hbm, rank_ref), (mask_hbm, mask_ref)), sems)
    lane = iota((tiles, 128), 1)
    cols = jnp.where(lane == 0, as_column(rank_ref[...].astype(F32)), 0.0).astype(BF16)
    spread = rows_of_tiles(rows, tiles)
    r = dot(spread, cols)[:, 0:1].astype(I32)
    column_tile = (z * depth + iota((depth, k_tiles), 0)) // tile_k
    select = jnp.where(column_tile == iota((depth, k_tiles), 1), 1.0, 0.0).astype(BF16)
    present = dot(select, mask_ref[...].astype(F32).astype(BF16)).astype(BF16)
    present = dot(present, spread, 1, 1)
    target = ((r + h) % 2) * half + (r // 2) * tile_rows + iota((rows, 1), 0) % tile_rows
    moved = jnp.where(target == iota((rows, half), 1), 1.0, 0.0).astype(BF16)
    for read in large:
        read.wait()
    masked = jnp.where(present > 0.5, amps_ref[...].astype(F32), 0.0).astype(BF16)
    code_ref[...] = encode(dot(masked, moved)).astype(jnp.int16)


def order(own, partner, rank, amp_mask, tile_k):
    k_width, rows = own.shape
    any_space = pl.BlockSpec(memory_space=pl.ANY)

    def kernel(*refs):
        order_kernel(tile_k, *refs)

    return pl.pallas_call(
        kernel,
        out_shape=jax.ShapeDtypeStruct((2 * k_width, rows // 2), jnp.int16),
        in_specs=[any_space] * 4,
        out_specs=pl.BlockSpec(memory_space=pltpu.VMEM),
        scratch_shapes=[
            pltpu.VMEM((2 * k_width, rows), BF16),
            pltpu.VMEM(rank.shape, I32),
            pltpu.VMEM(amp_mask.shape, I32),
            pltpu.SemaphoreType.DMA((4,)),
        ],
        compiler_params=pltpu.CompilerParams(vmem_limit_bytes=PREP_LIMIT << 20),
        name="order",
    )(own, partner, rank, amp_mask)


def place_tiles(slot, h, first, acc, out_ref, to):
    tile_rows = out_ref.shape[3]
    for n in range(acc.shape[0] // tile_rows):
        at = slot[0, 2 * (first + n) + h]
        tile = acc[n * tile_rows : (n + 1) * tile_rows] * (1.0 / 128.0)
        out_ref[to, at // 2, at % 2] = tile.astype(BF16)


def near_kernel(slot, code_ref, ints_ref, amps_ref, out_ref):
    depth, rows = code_ref.shape
    block = depth // 8
    for k in range(0, depth, block):
        amps_ref[:, k : k + block] = decode(code_ref[k : k + block]).T
    h = lax.axis_index("yhi").astype(I32)
    tall = rows // 4
    for r in range(0, rows, tall):
        acc = dot(amps_ref[r : r + tall], ints_ref[...])
        place_tiles(slot, h, r // out_ref.shape[3], acc, out_ref, h)


def near(slot, code, ints, owner_count, tile_rows):
    depth, rows = code.shape
    width = ints.shape[1]
    smem = pl.BlockSpec(memory_space=pltpu.SMEM)
    vmem = pl.BlockSpec(memory_space=pltpu.VMEM)
    return pl.pallas_call(
        near_kernel,
        out_shape=(
            jax.ShapeDtypeStruct((rows, depth), BF16),
            jax.ShapeDtypeStruct((2, owner_count, 2, tile_rows, width), BF16),
        ),
        in_specs=[smem, vmem, vmem],
        out_specs=(vmem, vmem),
        compiler_params=pltpu.CompilerParams(vmem_limit_bytes=NEAR_LIMIT << 20),
        cost_estimate=pl.CostEstimate(
            flops=2 * rows * depth * width, bytes_accessed=11 << 20, transcendentals=rows * depth
        ),
        name="near",
    )(slot, code, ints)


def far_kernel(slot, amps_ref, ints_hbm, _, out_ref, ints_ref, acc_ref, sems):
    h = lax.axis_index("yhi").astype(I32)
    rows, depth = amps_ref.shape
    parts = sems.shape[0]
    block = depth // parts
    reads = []
    for n in range(parts):
        at = pl.ds(n * block, block)
        reads.append(pltpu.make_async_copy(ints_hbm.at[at], ints_ref.at[at], sems.at[n]))
        reads[-1].start()
    tall = rows // 2
    for n in range(parts):
        reads[n].wait()
        at = pl.ds(n * block, block)
        for r in range(0, rows, tall):
            part = dot(amps_ref[r : r + tall, at], ints_ref[at])
            if n > 0:
                part += acc_ref[r : r + tall]
            if n < parts - 1:
                acc_ref[r : r + tall] = part
            else:
                place_tiles(slot, h, r // out_ref.shape[3], part, out_ref, 1 - h)


def far(slot, amps, ints, send):
    rows, depth = amps.shape
    width = ints.shape[1]
    smem = pl.BlockSpec(memory_space=pltpu.SMEM)
    vmem = pl.BlockSpec(memory_space=pltpu.VMEM)
    return pl.pallas_call(
        far_kernel,
        out_shape=jax.ShapeDtypeStruct(send.shape, BF16),
        in_specs=[smem, vmem, pl.BlockSpec(memory_space=pl.ANY), vmem],
        out_specs=vmem,
        scratch_shapes=[
            pltpu.VMEM(ints.shape, BF16),
            pltpu.VMEM((rows, width), F32),
            pltpu.SemaphoreType.DMA((3,)),
        ],
        input_output_aliases={3: 0},
        compiler_params=pltpu.CompilerParams(vmem_limit_bytes=FAR_LIMIT << 20),
        cost_estimate=pl.CostEstimate(
            flops=2 * rows * depth * width, bytes_accessed=8 << 20, transcendentals=0
        ),
        name="far",
    )(slot, amps, ints, send)


def update_kernel(recv_ref, meta_ref, mix_ref, vir_ref, out_ref, weight_ref, new_ref, sems):
    tile_rows = mix_ref.shape[1]
    tall = weight_ref.shape[0]
    batch = tall // (4 * tile_rows)
    copies = jnp.where(iota((tall, tile_rows), 0) % tile_rows == iota((tall, tile_rows), 1), 1.0, 0.0).astype(BF16)
    wide = dot(dot(copies, mix_ref[0]).astype(BF16), copies, 1, 1)
    same = iota((tall, tall), 0) // tile_rows == iota((tall, tall), 1) // tile_rows
    weight_ref[...] = jnp.where(same, wide, 0.0).astype(BF16)
    writes = []
    for step in range(meta_ref.shape[0] // batch):
        tiles, energies = [], []
        for s in range(step * batch, (step + 1) * batch):
            meta = meta_ref[s].astype(F32)
            odd = meta[0:1, 4:5] > 0.5
            for k in range(4):
                energy = meta[:, k : k + 1]
                even_tile = recv_ref[k % 2, s, k // 2].astype(F32)
                odd_tile = recv_ref[(k + 1) % 2, s, k // 2].astype(F32)
                tile = jnp.where(odd, odd_tile, even_tile)
                tiles.append(jnp.where(energy != 0.0, tile, 0.0).astype(BF16))
                energies.append(energy)
        mixed = dot(weight_ref[...], jnp.concatenate(tiles, axis=0))
        new = mixed / (vir_ref[...] - jnp.concatenate(energies, axis=0))
        at = pl.ds(step * batch * 4, batch * 4)
        new_ref[at] = new.astype(BF16).reshape((batch * 4,) + new_ref.shape[1:])
        write = pltpu.make_async_copy(new_ref.at[at], out_ref.at[at], sems.at[step])
        write.start()
        writes.append(write)
    for write in writes:
        write.wait()


def update(recv, meta, mix, vir_energy):
    _, owner_count, two, tile_rows, width = recv.shape
    batch = 2
    vmem = pl.BlockSpec(memory_space=pltpu.VMEM)
    return pl.pallas_call(
        update_kernel,
        out_shape=jax.ShapeDtypeStruct((owner_count * 4, tile_rows, width), BF16),
        in_specs=[vmem] * 4,
        out_specs=pl.BlockSpec(memory_space=pl.ANY),
        scratch_shapes=[
            pltpu.VMEM((batch * 4 * tile_rows, batch * 4 * tile_rows), BF16),
            pltpu.VMEM((owner_count * 4, tile_rows, width), BF16),
            pltpu.SemaphoreType.DMA((owner_count // batch,)),
        ],
        compiler_params=pltpu.CompilerParams(vmem_limit_bytes=24 << 20),
        name="update",
    )(recv, meta, mix, vir_energy)


def shards(amps, ints, amp_mask, keep_mask, owners, occ_energy, vir_energy, mix):
    tiles_dev, k_tiles = amp_mask.shape
    rows, k_width = amps.shape
    tile_rows = rows // tiles_dev
    depth, width = ints.shape
    owner_count = lax.axis_size(OCC)
    ints_far = lax.ppermute(ints, ("ylo", "yhi"), [(n, 3 - n) for n in range(4)])
    partner = lax.ppermute(amps, "yhi", [(0, 1), (1, 0)])
    rank, slot, meta = route(owners.T, keep_mask.T, occ_energy.reshape(8, rows // 8), owner_count)
    meta = lax.all_to_all(meta, OCC, 0, 0, tiled=True)
    code = order(amps.T, partner.T, rank, amp_mask.T, depth // k_tiles)
    code = lax.all_gather(code, "z", axis=0, tiled=True)
    decoded, send = near(slot, code, ints, owner_count, tile_rows)
    send = far(slot, decoded, ints_far, send)
    recv = lax.all_to_all(
        send.reshape(2 * owner_count, 2, tile_rows, width), ("yhi",) + OCC, 0, 0, tiled=True
    )
    recv = recv.reshape(2, owner_count, 2, tile_rows, width)
    return update(recv, meta, mix, vir_energy.reshape(1, width))


def solution(mesh):
    split = Mesh(mesh.devices.reshape(2, 4, 2, 16, 2), OCC + VIR)
    in_specs = (
        P(OCC, VIR),
        P(None, VIR),
        P(OCC, None),
        P(OCC, VIR),
        P(OCC, None),
        P(OCC),
        P(VIR),
        P(OCC, None, None),
    )
    return jax.shard_map(
        shards, mesh=split, in_specs=in_specs, out_specs=P(OCC, None, VIR), check_vma=False
    )
```
